128 devices in a mesh: section: 4 (over z), expert: 32 (over x, y, core).
Axes of the slice: x: 4, y: 4, z: 4, core: 2. Of those that a mesh axis runs over, the one named last changes fastest.
Arguments:
- inputs: bfloat16 [4, 1024, 3584], P(None, 'expert'), may hold values from -5 to 5
- routes: int32 [4, 4, 1024, 2], P('section', None, 'expert'), may hold values from 0 to 7, as said below
- norm_gain: bfloat16 [4, 3584], P('section'), may hold values from 0.099609375 to 1.8984375
- router: bfloat16 [4, 3584, 8], P('section'), may hold values from -0.0234375 to 0.0234375
- w_gate: bfloat16 [4, 3584, 19456], P('section', None, 'expert'), may hold values from -0.09375 to 0.09375
- w_up: bfloat16 [4, 3584, 19456], P('section', None, 'expert'), may hold values from -0.09375 to 0.09375
- w_down: bfloat16 [4, 19456, 3584], P('section', 'expert'), may hold values from -0.25 to 0.25
Outputs:
- outputs: bfloat16 [4, 1024, 3584], P(None, 'expert', 'section')
The draws below stay inside these ranges and needn't reach their ends.
Inputs may be any that keep to these rules, and one draw needn't show every extreme that they name: `routes`: for each layer and micro-batch, the rows of one index of expert (32 tokens, two choices each) name each expert at most 9 times; a token's two ids differ.
All inputs are finite; a program needn't handle non-finite values.
Results may differ from the reference program's by a relative error of at most 0.024.
Values may be sent and summed in bfloat16 or wider, within the bound.
A program may use at most 128 MiB of HBM per device.

```python
import jax
import jax.numpy as jnp
from jax import lax

D = 3584
EH = 2432
EXPERTS = 8
TOK_DEV = 32
MICRO = 4
GROUP = 4
EH_DEV = 608
LAYERS = 4
TOKENS = 1024
CAP = 9
N_EXPERT = 32


def draw_routes(key, part):
    key = jax.random.fold_in(key, 11)
    device_blocks = TOKENS // TOK_DEV
    hot_keys = jax.random.split(jax.random.fold_in(key, 1), LAYERS * MICRO)
    hottest = jax.vmap(lambda single: jax.random.randint(single, (), 0, EXPERTS, dtype=jnp.int32))(hot_keys)
    hottest = jnp.repeat(hottest, device_blocks)
    block_keys = jax.random.split(jax.random.fold_in(key, 2), LAYERS * MICRO * device_blocks)

    def one_block(single, hot_expert):
        first_key, second_key, third_key = jax.random.split(single, 3)
        tickets = jnp.arange((EXPERTS - 1) * CAP, dtype=jnp.int32) // CAP
        others = tickets + (tickets >= hot_expert).astype(jnp.int32)
        shuffled = jax.random.permutation(first_key, (EXPERTS - 1) * CAP)
        picked = jnp.sort(others[shuffled][:2 * TOK_DEV - CAP])
        sequence = jnp.concatenate([jnp.full((CAP,), hot_expert, jnp.int32), picked])
        leading = sequence[:TOK_DEV]
        trailing = sequence[TOK_DEV:]
        order = jax.random.permutation(second_key, TOK_DEV)
        leading = leading[order]
        trailing = trailing[order]
        flipped = jax.random.randint(third_key, (TOK_DEV,), 0, 2, dtype=jnp.int32)
        first_col = jnp.where(flipped == 1, trailing, leading)
        second_col = jnp.where(flipped == 1, leading, trailing)
        return jnp.stack([first_col, second_col], axis=-1)
    blocks = jax.vmap(one_block)(block_keys, hottest)
    return blocks.reshape(LAYERS, MICRO, TOKENS, 2).astype(jnp.int32)


def level_of(stream_key, extent, shards, low, largest):
    factor_of, own = 1.0, jax.random.fold_in(stream_key, 6)
    for position, parts in shards:
        draws = jnp.exp(jax.random.uniform(jax.random.fold_in(own, position), (parts,), jnp.float32, low / len(shards), largest / len(shards)))
        factor_of = factor_of * jnp.repeat(draws, extent[position] // parts).reshape([-1 if axis == position else 1 for axis in range(len(extent))])
    return factor_of


def scatter_about(stream_key, dims, spread, reach, pieces=(), kind=jnp.bfloat16):
    level = level_of(stream_key, dims, pieces, -0.22, 0.18) if pieces else 1.0
    drawn = jax.random.normal(stream_key, dims, jnp.float32) * spread * level
    return jnp.minimum(jnp.maximum(drawn, -reach), reach).astype(kind)


def setup_inputs(seed: int = 0) -> dict:
    streams_of = jax.random.split(jax.random.key(seed), 8)
    return {
        "inputs": scatter_about(streams_of[0], (MICRO, TOKENS, D), 1.0, 5.0, ((1, 32),)),
        "routes": draw_routes(jax.random.fold_in(streams_of[7], 71), 0),
        "norm_gain": jnp.clip(1.0 + 0.18 * jax.random.normal(streams_of[2], (LAYERS, D), jnp.float32), 0.099609375, 1.8984375).astype(jnp.bfloat16),
        "router": scatter_about(streams_of[3], (LAYERS, D, EXPERTS), (16 * D) ** -0.5, 0.0234375, ((0, 4),)),
        "w_gate": scatter_about(streams_of[4], (LAYERS, D, EXPERTS * EH), D ** -0.5, 0.09375, ((0, 4), (2, 32))),
        "w_up": scatter_about(streams_of[5], (LAYERS, D, EXPERTS * EH), D ** -0.5, 0.09375, ((0, 4), (2, 32))),
        "w_down": scatter_about(streams_of[6], (LAYERS, EXPERTS * EH, D), (EH // 4) ** -0.5, 0.25, ((0, 4), (1, 32))),
    }


EPSILON = 1e-06

def normalized(hidden, gain):
    widened = hidden.astype(jnp.float32)
    meansq = lax.optimization_barrier(jnp.mean(widened * widened, axis=-1, keepdims=True))
    return (widened, (widened * lax.rsqrt(meansq + EPSILON) * gain.astype(jnp.float32)).astype(jnp.bfloat16))

def expert_rows(arrived, gate_block, up_block, down_block):
    gate_part = jnp.dot(arrived, gate_block, preferred_element_type=jnp.float32)
    upward = jnp.dot(arrived, up_block, preferred_element_type=jnp.float32)
    between = (jax.nn.silu(gate_part) * upward).astype(jnp.bfloat16)
    total = jnp.zeros((arrived.shape[0], down_block.shape[1]), jnp.float32)
    for member in range(GROUP):
        lower = member * EH_DEV
        partial_out = jnp.dot(between[:, lower:lower + EH_DEV], down_block[lower:lower + EH_DEV], preferred_element_type=jnp.float32).astype(jnp.bfloat16)
        partial_out = lax.optimization_barrier(partial_out)
        total = total + partial_out.astype(jnp.float32)
    return total

def moe_layer(hidden, chosen, gain, columns, gate_all, up_all, down_all):
    widened, normed = normalized(hidden, gain)
    logits = jnp.dot(normed, columns, preferred_element_type=jnp.float32)
    first_logit = jnp.take_along_axis(logits, chosen[:, 0:1], axis=1)[:, 0]
    second_logit = jnp.take_along_axis(logits, chosen[:, 1:2], axis=1)[:, 0]
    first_weight = jax.nn.sigmoid(first_logit - second_logit)
    second_weight = 1.0 - first_weight
    flat_choice = jnp.concatenate([chosen[:, 0], chosen[:, 1]]).astype(jnp.int32)
    flat_rows = jnp.concatenate([normed, normed], axis=0)
    total_rows = flat_choice.shape[0]
    feature_count = hidden.shape[1]

    def per_expert(operand):
        expert, gate_block, up_block, down_block = operand
        picked = jnp.nonzero(flat_choice == expert, size=N_EXPERT * CAP, fill_value=total_rows)[0].astype(jnp.int32)
        gathered = jnp.take(flat_rows, picked, axis=0, mode='clip')
        return (picked, expert_rows(gathered, gate_block, up_block, down_block))
    positions, answers = lax.map(per_expert, (jnp.arange(EXPERTS, dtype=jnp.int32), gate_all, up_all, down_all))
    routed = jnp.zeros((total_rows, feature_count), jnp.float32)
    routed = routed.at[positions.reshape(-1)].set(answers.reshape(-1, feature_count), mode='drop')
    first_out = routed[:TOKENS]
    second_out = routed[TOKENS:]
    updated = widened + first_weight[:, None] * first_out + second_weight[:, None] * second_out
    return updated.astype(jnp.bfloat16)

def reference(inputs, routes, norm_gain, router, w_gate, w_up, w_down):
    results = []
    for batch_index in range(MICRO):
        hidden = inputs[batch_index]
        for layer_index in range(LAYERS):
            gate_all = jnp.transpose(w_gate[layer_index].reshape(D, EXPERTS, EH), (1, 0, 2))
            up_all = jnp.transpose(w_up[layer_index].reshape(D, EXPERTS, EH), (1, 0, 2))
            down_all = w_down[layer_index].reshape(EXPERTS, EH, D)
            hidden = moe_layer(hidden, routes[layer_index, batch_index], norm_gain[layer_index], router[layer_index], gate_all, up_all, down_all)
        results.append(hidden)
    return jnp.stack(results)
```

```python
import functools

import numpy as np
import jax
import jax.numpy as jnp
from jax import lax
from jax.experimental import pallas as pl
from jax.experimental.pallas import tpu as pltpu
from jax.sharding import PartitionSpec as P

EPSILON = 1e-06
MESH = pl.DeviceIdType.MESH
F32 = jnp.float32
BF16 = jnp.bfloat16

CAP = 9
WIDE = 512
PIECES = 7
BLOCK = 64
SOURCES = 8
PACKED = 80
CHIPS = 16


def selection():
    table = np.zeros((PIECES * PACKED, SOURCES * BLOCK), np.float32)
    for piece in range(PIECES):
        for source in range(SOURCES):
            for slot in range(CAP):
                table[
                    piece * PACKED + source * CAP + slot, source * BLOCK + piece * CAP + slot
                ] = 1.0
    return table


def kernel(
    inputs, routes, routes_row, gain, router, gate_in, up_in, down_in, sel, unsel,
    out,
    w_gate, w_up, w_down, hid, d_out, held, packed, answers, own_sum, sib_out, sib_in,
    ret_out, came, weight_hi, weight_lo, h_out,
    w_sem, h_sem, d_sem, sib_sem, ret_sem, out_sem,
    d_sent, f_sent, sib_sent, ret_sent, h_sent,
):
    micros, tokens, _ = inputs.shape
    units = 2 * micros
    section = lax.axis_index("section")
    place = lax.axis_index("expert")
    sections = 4
    core = lax.rem(place, 2)
    chip = place // 2
    side = chip // 8
    sibling = (section, chip * 2 + (1 - core))

    weight_copies = [
        pltpu.make_async_copy(gate_in, w_gate, w_sem.at[0]),
        pltpu.make_async_copy(up_in, w_up, w_sem.at[1]),
        pltpu.make_async_copy(down_in, w_down, w_sem.at[2]),
    ]

    def input_copy(m):
        return pltpu.make_async_copy(inputs.at[m], hid.at[m], h_sem.at[m])

    def relay_copy(m):
        return pltpu.make_async_remote_copy(
            h_out.at[m], hid.at[m], h_sent, h_sem.at[m],
            device_id=(lax.rem(section + 1, sections), place), device_id_type=MESH,
        )

    @pl.when(section == 0)
    def _():
        for m in range(micros):
            input_copy(m).start()

    barrier = pltpu.get_barrier_semaphore()

    def greet(step, carry):
        pl.semaphore_signal(
            barrier, inc=1, device_id=(section, lax.rem(place + step, 32)), device_id_type=MESH
        )
        return carry

    lax.fori_loop(1, 32, greet, 0)
    for step in range(1, sections):
        pl.semaphore_signal(
            barrier, inc=1, device_id=(lax.rem(section + step, sections), place),
            device_id_type=MESH,
        )
    for copy in weight_copies:
        copy.start()
    pl.semaphore_wait(barrier, 31 + sections - 1)

    def dispatch_copy(m, expert, to, source):
        return pltpu.make_async_remote_copy(
            d_out.at[m, pl.ds(pl.multiple_of(expert * BLOCK, BLOCK), BLOCK)],
            held.at[2 * m + core, source],
            d_sent, d_sem.at[2 * m + core, source],
            device_id=(section, to * 2 + side), device_id_type=MESH,
        )

    def dispatch_stay(m):
        return pltpu.make_async_copy(
            d_out.at[m, pl.ds(pl.multiple_of((chip // 2) * BLOCK, BLOCK), BLOCK)],
            held.at[2 * m + core, chip], d_sem.at[2 * m + core, chip],
        )

    def dispatch(m):
        input_copy(m).wait()
        hidden = hid[m].astype(F32)
        meansq = jnp.mean(hidden * hidden, axis=-1, keepdims=True)
        normed = (hidden * lax.rsqrt(meansq + EPSILON) * gain[...].astype(F32)).astype(BF16)
        stacked = jnp.concatenate(
            [normed[:, k * WIDE:(k + 1) * WIDE] for k in range(PIECES)], axis=0
        )
        chosen = routes[m]
        first, second = chosen[:, 0:1], chosen[:, 1:2]
        along = routes_row[m]
        first_row, second_row = along[0:1], along[1:2]
        width = PIECES * tokens
        up_down = lax.broadcasted_iota(jnp.int32, (tokens, width), 0)
        left_right = lax.broadcasted_iota(jnp.int32, (tokens, width), 1)
        token_of = lax.rem(left_right, tokens)
        earlier = up_down < token_of

        def total(condition, axis):
            return jnp.sum(jnp.where(condition, 1, 0), axis=axis, keepdims=True)

        slot_first = total((first == first_row) & earlier, 0)
        slot_second = total(first == second_row, 0) + total((second == second_row) & earlier, 0)
        piece_row = lax.broadcasted_iota(jnp.int32, (1, width), 1) // tokens * CAP
        target_first = first_row * BLOCK + piece_row + slot_first
        target_second = second_row * BLOCK + piece_row + slot_second
        rows = lax.broadcasted_iota(jnp.int32, (8 * BLOCK, width), 0)
        placing = jnp.where((rows == target_first) | (rows == target_second), 1.0, 0.0)
        outgoing = jnp.dot(placing.astype(BF16), stacked, preferred_element_type=F32)
        d_out[m] = outgoing.astype(BF16)

        def send(step, carry):
            to = lax.rem(chip + step, CHIPS)
            dispatch_copy(m, to // 2, to, chip).start()
            return carry

        lax.fori_loop(1, CHIPS, send, 0)

        @pl.when(side == core)
        def _():
            dispatch_stay(m).start()

        @pl.when(side != core)
        def _():
            dispatch_copy(m, chip // 2, chip, chip).start()

        logits = jnp.dot(normed, router[...], preferred_element_type=F32)
        expert_range = lax.broadcasted_iota(jnp.int32, logits.shape, 1)
        first_logit = jnp.sum(jnp.where(first == expert_range, logits, 0.0), axis=1, keepdims=True)
        second_logit = jnp.sum(
            jnp.where(second == expert_range, logits, 0.0), axis=1, keepdims=True
        )
        first_weight = 1.0 / (1.0 + jnp.exp(second_logit - first_logit))
        second_weight = 1.0 - first_weight
        before = (left_right < up_down) & (left_right < tokens)
        own_first = total((first == first_row) & before, 1)
        own_second = total((second == first_row) & (left_right < tokens), 1) + total(
            (second == second_row) & before, 1
        )
        at_first = first * BLOCK + own_first
        at_second = second * BLOCK + own_second
        column = lax.broadcasted_iota(jnp.int32, (tokens, CHIPS * BLOCK), 1)
        column = column // (2 * BLOCK) * BLOCK + lax.rem(column, BLOCK)
        for k in range(PIECES):
            weights = jnp.where(column == at_first + k * CAP, first_weight, 0.0) + jnp.where(
                column == at_second + k * CAP, second_weight, 0.0
            )
            high = weights.astype(BF16)
            weight_hi[k * tokens:(k + 1) * tokens, :] = high
            weight_lo[k * tokens:(k + 1) * tokens, :] = (weights - high.astype(F32)).astype(BF16)

    def block_arrival(u, source):
        return pltpu.make_async_copy(
            held.at[u, source], held.at[u, source], d_sem.at[u, source]
        )

    def forward_copy(u, source):
        return pltpu.make_async_remote_copy(
            held.at[u, source], held.at[u, source], f_sent, d_sem.at[u, source],
            device_id=sibling, device_id_type=MESH,
        )

    def sibling_copy(u):
        return pltpu.make_async_remote_copy(
            sib_out.at[u], sib_in.at[u], sib_sent, sib_sem.at[u],
            device_id=sibling, device_id_type=MESH,
        )

    def return_copy(u, k):
        home = core * SOURCES + k
        return pltpu.make_async_remote_copy(
            ret_out.at[u, k], came.at[u // 2, chip], ret_sent, ret_sem.at[u // 2, chip],
            device_id=(section, home * 2 + lax.rem(u, 2)), device_id_type=MESH,
        )

    def return_stay(u, k):
        return pltpu.make_async_copy(
            ret_out.at[u, k], came.at[u // 2, chip], ret_sem.at[u // 2, chip]
        )

    def stays(u, k):
        return (core * SOURCES + k == chip) & (lax.rem(u, 2) == core)

    def select(u, base):
        blocks = held[u, pl.ds(base, SOURCES)].reshape(SOURCES * BLOCK, WIDE)
        return jnp.dot(sel[...], blocks, preferred_element_type=F32).astype(BF16)

    def compute(u):
        own, other = core * SOURCES, (1 - core) * SOURCES

        def pass_on(k, carry):
            block_arrival(u, own + k).wait()
            forward_copy(u, own + k).start()
            return carry

        lax.fori_loop(0, SOURCES, pass_on, 0)
        mine = select(u, own)
        for k in range(PIECES):
            packed[0:PACKED, k * WIDE:(k + 1) * WIDE] = mine[k * PACKED:(k + 1) * PACKED]

        def arrive(k, carry):
            block_arrival(u, other + k).wait()
            return carry

        lax.fori_loop(0, SOURCES, arrive, 0)
        theirs = select(u, other)
        for k in range(PIECES):
            packed[PACKED:, k * WIDE:(k + 1) * WIDE] = theirs[k * PACKED:(k + 1) * PACKED]
        rows = packed[...]
        gated = jnp.dot(rows, w_gate[...], preferred_element_type=F32)
        upward = jnp.dot(rows, w_up[...], preferred_element_type=F32)
        between = (gated / (1.0 + jnp.exp(-gated)) * upward).astype(BF16)
        for k in range(PIECES):
            part = jnp.dot(
                between, w_down[:, k * WIDE:(k + 1) * WIDE], preferred_element_type=F32
            ).astype(BF16)
            answers[0, k * PACKED:(k + 1) * PACKED] = part[:PACKED]
            answers[1, k * PACKED:(k + 1) * PACKED] = part[PACKED:]
        sib_out[u] = jnp.dot(unsel[...], answers[1], preferred_element_type=F32).astype(BF16)
        sibling_copy(u).start()
        own_sum[...] = jnp.dot(unsel[...], answers[0], preferred_element_type=F32)
        sibling_copy(u).wait_recv()
        summed = (own_sum[...] + sib_in[u].astype(F32)).astype(BF16)
        ret_out[u] = summed.reshape(SOURCES, BLOCK, WIDE)

        def send(k, carry):
            @pl.when(stays(u, k))
            def _():
                return_stay(u, k).start()

            @pl.when(jnp.logical_not(stays(u, k)))
            def _():
                return_copy(u, k).start()

            return carry

        lax.fori_loop(0, SOURCES, send, 0)

    def out_copy(m, to):
        return pltpu.make_async_remote_copy(
            h_out.at[m, :, to * 896:(to + 1) * 896], out.at[m], h_sent, out_sem.at[m],
            device_id=(to, place), device_id_type=MESH,
        )

    def out_stay(m):
        return pltpu.make_async_copy(
            h_out.at[m, :, 3 * 896:4 * 896], out.at[m], out_sem.at[m]
        )

    def combine(m):
        def arrive(k, carry):
            pltpu.make_async_copy(came.at[m, k], came.at[m, k], ret_sem.at[m, k]).wait()
            return carry

        lax.fori_loop(0, CHIPS, arrive, 0)
        answered = came[m].reshape(CHIPS * BLOCK, WIDE)
        added = jnp.dot(weight_hi[...], answered, preferred_element_type=F32) + jnp.dot(
            weight_lo[...], answered, preferred_element_type=F32
        )
        for k in range(PIECES):
            at = slice(k * WIDE, (k + 1) * WIDE)
            h_out[m, :, at] = (
                hid[m, :, at].astype(F32) + added[k * tokens:(k + 1) * tokens]
            ).astype(BF16)

        @pl.when(section < sections - 1)
        def _():
            relay_copy(m).start()

        @pl.when(section == sections - 1)
        def _():
            for to in range(sections - 1):
                out_copy(m, to).start()
            out_stay(m).start()

    @pl.when(core == 0)
    def _():
        dispatch(0)

    for copy in weight_copies:
        copy.wait()

    def step(u, carry):
        compute(u)

        @pl.when((lax.rem(u + 1, 2) == core) & (u + 1 < units))
        def _():
            dispatch((u + 1) // 2)

        @pl.when(lax.rem(u, 2) == core)
        def _():
            combine(u // 2)

        return carry

    lax.fori_loop(0, units, step, 0)

    def drain(m, carry):
        def drain_dispatch(step, inner):
            to = lax.rem(chip + step, CHIPS)
            dispatch_copy(m, to // 2, to, chip).wait_send()
            return inner

        lax.fori_loop(1, CHIPS, drain_dispatch, 0)

        @pl.when(side != core)
        def _():
            dispatch_copy(m, chip // 2, chip, chip).wait_send()

        for half in range(2):
            u = 2 * m + half
            sibling_copy(u).wait_send()

            def drain_unit(k, inner):
                forward_copy(u, core * SOURCES + k).wait_send()

                @pl.when(jnp.logical_not(stays(u, k)))
                def _():
                    return_copy(u, k).wait_send()

                return inner

            lax.fori_loop(0, SOURCES, drain_unit, 0)

        @pl.when(section < sections - 1)
        def _():
            relay_copy(m).wait_send()

        @pl.when(section == sections - 1)
        def _():
            for to in range(sections - 1):
                out_copy(m, to).wait_send()

        out_stay(m).wait()
        return carry

    lax.fori_loop(0, micros, drain, 0)


def on_device(inputs, routes, norm_gain, router, w_gate, w_up, w_down):
    micros, tokens, features = inputs.shape
    units = 2 * micros
    hidden_units = w_gate.shape[2]
    table = selection()
    sel = jnp.asarray(table, BF16)
    unsel = jnp.asarray(table.T, BF16)
    routes_row = jnp.tile(jnp.swapaxes(routes[0], 1, 2), (1, 1, PIECES))
    vmem = pl.BlockSpec(memory_space=pltpu.VMEM)
    anywhere = pl.BlockSpec(memory_space=pl.ANY)
    dma = pltpu.SemaphoreType.DMA
    return pl.pallas_call(
        kernel,
        out_shape=jax.ShapeDtypeStruct((micros, tokens, features // 4), BF16),
        in_specs=[anywhere, vmem, vmem, vmem, vmem, anywhere, anywhere, anywhere, vmem, vmem],
        out_specs=vmem,
        scratch_shapes=[
            pltpu.VMEM((features, hidden_units), BF16),
            pltpu.VMEM((features, hidden_units), BF16),
            pltpu.VMEM((hidden_units, features), BF16),
            pltpu.VMEM((micros, tokens, features), BF16),
            pltpu.VMEM((micros, 8 * BLOCK, WIDE), BF16),
            pltpu.VMEM((units, CHIPS, BLOCK, WIDE), BF16),
            pltpu.VMEM((2 * PACKED, features), BF16),
            pltpu.VMEM((2, PIECES * PACKED, WIDE), BF16),
            pltpu.VMEM((SOURCES * BLOCK, WIDE), F32),
            pltpu.VMEM((units, SOURCES * BLOCK, WIDE), BF16),
            pltpu.VMEM((units, SOURCES * BLOCK, WIDE), BF16),
            pltpu.VMEM((units, SOURCES, BLOCK, WIDE), BF16),
            pltpu.VMEM((micros, CHIPS, BLOCK, WIDE), BF16),
            pltpu.VMEM((PIECES * tokens, CHIPS * BLOCK), BF16),
            pltpu.VMEM((PIECES * tokens, CHIPS * BLOCK), BF16),
            pltpu.VMEM((micros, tokens, features), BF16),
            dma((3,)),
            dma((micros,)),
            dma((units, CHIPS)),
            dma((units,)),
            dma((micros, CHIPS)),
            dma((micros,)),
            dma, dma, dma, dma, dma,
        ],
        compiler_params=pltpu.CompilerParams(
            collective_id=0, has_side_effects=True, vmem_limit_bytes=60 * 2**20
        ),
        name="moe_relay",
    )(
        inputs, routes[0], routes_row, norm_gain, router[0], w_gate[0], w_up[0], w_down[0],
        sel, unsel,
    )


def solution(mesh):
    return jax.shard_map(
        on_device,
        mesh=mesh,
        in_specs=(
            P(None, "expert", None),
            P("section", None, "expert", None),
            P("section", None),
            P("section", None, None),
            P("section", None, "expert"),
            P("section", None, "expert"),
            P("section", "expert", None),
        ),
        out_specs=P(None, "expert", "section"),
        check_vma=False,
    )
```

```python
import jax
import jax.numpy as jnp
from jax import lax
from jax.experimental import pallas as pl
from jax.experimental.pallas import tpu as pltpu
from jax.sharding import PartitionSpec as P

EPSILON = 1e-06
MESH = pl.DeviceIdType.MESH
F32 = jnp.float32
BF16 = jnp.bfloat16

CAP = 9
WIDE = 512
PIECES = 7
HALF = 1792
NARROW = 256
BLOCK = 64
SOURCES = 8
PACKED = 80
CHIPS = 16
AHEAD = 2
BEHIND = 1


def fill_selection(sel, unsel):
    down = lax.broadcasted_iota(jnp.int32, (PIECES * PACKED, 1), 0)
    piece, rest = down // PACKED, lax.rem(down, PACKED)
    source, slot = rest // CAP, lax.rem(rest, CAP)
    taken = jnp.where(rest < SOURCES * CAP, source * BLOCK + piece * CAP + slot, -1)
    sel[...] = jnp.where(
        lax.broadcasted_iota(jnp.int32, sel.shape, 1) == taken, 1.0, 0.0
    ).astype(BF16)
    down = lax.broadcasted_iota(jnp.int32, (SOURCES * BLOCK, 1), 0)
    source, rest = down // BLOCK, lax.rem(down, BLOCK)
    piece, slot = rest // CAP, lax.rem(rest, CAP)
    taken = jnp.where(piece < PIECES, piece * PACKED + source * CAP + slot, -1)
    unsel[...] = jnp.where(
        lax.broadcasted_iota(jnp.int32, unsel.shape, 1) == taken, 1.0, 0.0
    ).astype(BF16)


def dot_nt(rows, columns):
    return lax.dot_general(
        rows, columns, (((1,), (1,)), ((), ())), preferred_element_type=F32
    )


def kernel(
    inputs, routes, gain, router, gate_in, up_in, down_in,
    out,
    w_gate, w_up, w_down, sel, unsel, hid, placing, d_out, held, packed, mid_out, mid_in, partial,
    answers, ret_out, came, weight_hi, weight_lo, h_out,
    w_sem, h_sem, d_sem, mid_sem, ret_sem, out_sem,
    swap_sent, d_sent, f_sent, mid_sent, ret_sent, h_sent,
):
    micros, tokens, _ = inputs.shape
    units = 2 * micros
    section = lax.axis_index("section")
    place = lax.axis_index("expert")
    sections = 4
    core = lax.rem(place, 2)
    chip = place // 2
    side = chip // 8
    sibling = (section, chip * 2 + (1 - core))

    def down_half(half):
        return down_in.at[:, pl.ds(pl.multiple_of(half * HALF, HALF), HALF)]

    swap_copy = pltpu.make_async_remote_copy(
        down_half(1 - core), w_down.at[1], swap_sent, w_sem.at[3],
        device_id=sibling, device_id_type=MESH,
    )
    weight_copies = [
        pltpu.make_async_copy(gate_in, w_gate, w_sem.at[0]),
        pltpu.make_async_copy(up_in, w_up, w_sem.at[1]),
        pltpu.make_async_copy(down_half(core), w_down.at[0], w_sem.at[2]),
    ]

    def input_copy(m):
        return pltpu.make_async_copy(inputs.at[m], hid.at[m], h_sem.at[m])

    def relay_copy(m, half):
        at = slice(half * HALF, (half + 1) * HALF)
        return pltpu.make_async_remote_copy(
            h_out.at[m, :, at], hid.at[m, :, at], h_sent, h_sem.at[m],
            device_id=(lax.rem(section + 1, sections), place), device_id_type=MESH,
        )

    @pl.when(section == 0)
    def _():
        for m in range(micros):
            input_copy(m).start()

    barrier = pltpu.get_barrier_semaphore()

    def greet(step, carry):
        pl.semaphore_signal(
            barrier, inc=1, device_id=(section, lax.rem(place + step, 32)), device_id_type=MESH
        )
        return carry

    lax.fori_loop(1, 32, greet, 0)
    for step in range(1, sections):
        pl.semaphore_signal(
            barrier, inc=1, device_id=(lax.rem(section + step, sections), place),
            device_id_type=MESH,
        )
    for copy in weight_copies:
        copy.start()
    fill_selection(sel, unsel)
    pl.semaphore_wait(barrier, 31 + sections - 1)
    swap_copy.start()

    def dispatch_copy(m, expert, to, source):
        return pltpu.make_async_remote_copy(
            d_out.at[m, pl.ds(pl.multiple_of(expert * BLOCK, BLOCK), BLOCK)],
            held.at[2 * m + core, source],
            d_sent, d_sem.at[2 * m + core, source],
            device_id=(section, to * 2 + side), device_id_type=MESH,
        )

    def dispatch_stay(m):
        return pltpu.make_async_copy(
            d_out.at[m, pl.ds(pl.multiple_of((chip // 2) * BLOCK, BLOCK), BLOCK)],
            held.at[2 * m + core, chip], d_sem.at[2 * m + core, chip],
        )

    def dispatch(m):
        width = PIECES * tokens
        up_down = lax.broadcasted_iota(jnp.int32, (tokens, width), 0)
        left_right = lax.broadcasted_iota(jnp.int32, (tokens, width), 1)
        token_of = lax.rem(left_right, tokens)
        chosen = routes[m]
        square = up_down[:, :tokens] == left_right[:, :tokens]
        first = jnp.sum(jnp.where(square, chosen[0:1], 0), axis=1, keepdims=True)
        second = jnp.sum(jnp.where(square, chosen[1:2], 0), axis=1, keepdims=True)
        repeat = up_down == token_of
        first_row = jnp.sum(jnp.where(repeat, first, 0), axis=0, keepdims=True)
        second_row = jnp.sum(jnp.where(repeat, second, 0), axis=0, keepdims=True)
        earlier = up_down < token_of

        def total(condition, axis):
            return jnp.sum(jnp.where(condition, 1, 0), axis=axis, keepdims=True)

        slot_first = total((first == first_row) & earlier, 0)
        slot_second = total(first == second_row, 0) + total((second == second_row) & earlier, 0)
        piece_row = lax.broadcasted_iota(jnp.int32, (1, width), 1) // tokens * CAP
        target_first = first_row * BLOCK + piece_row + slot_first
        target_second = second_row * BLOCK + piece_row + slot_second
        rows = lax.broadcasted_iota(jnp.int32, (8 * BLOCK, width), 0)
        placing[...] = jnp.where(
            (rows == target_first) | (rows == target_second), 1.0, 0.0
        ).astype(BF16)

        input_copy(m).wait()
        hidden = hid[m].astype(F32)
        meansq = jnp.mean(hidden * hidden, axis=-1, keepdims=True)
        normed = (hidden * lax.rsqrt(meansq + EPSILON) * gain[...].astype(F32)).astype(BF16)
        stacked = jnp.concatenate(
            [normed[:, k * WIDE:(k + 1) * WIDE] for k in range(PIECES)], axis=0
        )
        d_out[m] = jnp.dot(placing[...], stacked, preferred_element_type=F32).astype(BF16)

        def send(step, carry):
            to = lax.rem(chip + step, CHIPS)
            dispatch_copy(m, to // 2, to, chip).start()
            return carry

        lax.fori_loop(1, CHIPS, send, 0)

        @pl.when(side == core)
        def _():
            dispatch_stay(m).start()

        @pl.when(side != core)
        def _():
            dispatch_copy(m, chip // 2, chip, chip).start()

        logits = dot_nt(normed, router[...])
        expert_range = lax.broadcasted_iota(jnp.int32, logits.shape, 1)
        first_logit = jnp.sum(jnp.where(first == expert_range, logits, 0.0), axis=1, keepdims=True)
        second_logit = jnp.sum(
            jnp.where(second == expert_range, logits, 0.0), axis=1, keepdims=True
        )
        first_weight = 1.0 / (1.0 + jnp.exp(second_logit - first_logit))
        second_weight = 1.0 - first_weight
        before = (left_right < up_down) & (left_right < tokens)
        own_first = total((first == first_row) & before, 1)
        own_second = total((second == first_row) & (left_right < tokens), 1) + total(
            (second == second_row) & before, 1
        )
        at_first = first * BLOCK + own_first
        at_second = second * BLOCK + own_second
        column = lax.broadcasted_iota(jnp.int32, (tokens, CHIPS * BLOCK), 1)
        column = column // (2 * BLOCK) * BLOCK + lax.rem(column, BLOCK)
        for k in range(PIECES):
            weights = jnp.where(column == at_first + k * CAP, first_weight, 0.0) + jnp.where(
                column == at_second + k * CAP, second_weight, 0.0
            )
            high = weights.astype(BF16)
            weight_hi[lax.rem(m, 2), k * tokens:(k + 1) * tokens] = high
            weight_lo[lax.rem(m, 2), k * tokens:(k + 1) * tokens] = (
                weights - high.astype(F32)
            ).astype(BF16)

    def block_arrival(u, source):
        return pltpu.make_async_copy(
            held.at[u, source], held.at[u, source], d_sem.at[u, source]
        )

    def forward_copy(u, source):
        return pltpu.make_async_remote_copy(
            held.at[u, source], held.at[u, source], f_sent, d_sem.at[u, source],
            device_id=sibling, device_id_type=MESH,
        )

    def between_copy(u, half):
        there, here = slice(half * PACKED, (half + 1) * PACKED), slice(
            (1 - half) * PACKED, (2 - half) * PACKED
        )
        return pltpu.make_async_remote_copy(
            mid_out.at[u, there], mid_in.at[u, here], mid_sent, mid_sem.at[u],
            device_id=sibling, device_id_type=MESH,
        )

    def between_arrival(u):
        return pltpu.make_async_copy(mid_in.at[u], mid_in.at[u], mid_sem.at[u])

    def return_copy(u, home):
        return pltpu.make_async_remote_copy(
            ret_out.at[u, home], came.at[u // 2, core, chip], ret_sent,
            ret_sem.at[u // 2, core, chip],
            device_id=(section, home * 2 + lax.rem(u, 2)), device_id_type=MESH,
        )

    def return_stay(u):
        return pltpu.make_async_copy(
            ret_out.at[u, chip], came.at[u // 2, core, chip], ret_sem.at[u // 2, core, chip]
        )

    def stays(u, home):
        return (home == chip) & (lax.rem(u, 2) == core)

    def select(u, base):
        blocks = held[u, pl.ds(base, SOURCES)].reshape(SOURCES * BLOCK, WIDE)
        return jnp.dot(sel[...], blocks, preferred_element_type=F32).astype(BF16)

    def compute(u):
        own, other = core * SOURCES, (1 - core) * SOURCES

        def pass_on(k, carry):
            block_arrival(u, own + k).wait()
            forward_copy(u, own + k).start()
            return carry

        lax.fori_loop(0, SOURCES, pass_on, 0)
        mine = select(u, own)
        for k in range(PIECES):
            packed[0:PACKED, k * WIDE:(k + 1) * WIDE] = mine[k * PACKED:(k + 1) * PACKED]

        def arrive(k, carry):
            block_arrival(u, other + k).wait()
            return carry

        lax.fori_loop(0, SOURCES, arrive, 0)
        theirs = select(u, other)
        for k in range(PIECES):
            packed[PACKED:, k * WIDE:(k + 1) * WIDE] = theirs[k * PACKED:(k + 1) * PACKED]
        rows = packed[...]
        gated = dot_nt(rows, w_gate[...])
        upward = dot_nt(rows, w_up[...])
        between = (gated / (1.0 + jnp.exp(-gated)) * upward).astype(BF16)
        mid_out[u] = between
        for half in range(2):
            between_copy(u, half).start()
        partial[...] = jnp.dot(between, w_down[0], preferred_element_type=F32)
        between_arrival(u).wait()
        theirs = mid_in[u]
        for k in range(PIECES):
            at = slice(k * NARROW, (k + 1) * NARROW)
            part = partial[:, at] + jnp.dot(
                theirs, w_down[1, :, at], preferred_element_type=F32
            )
            part = part.astype(BF16)
            answers[0, k * PACKED:(k + 1) * PACKED] = part[:PACKED]
            answers[1, k * PACKED:(k + 1) * PACKED] = part[PACKED:]
        for group, base in ((0, own), (1, other)):
            blocks = jnp.dot(unsel[...], answers[group], preferred_element_type=F32)
            ret_out[u, pl.ds(base, SOURCES)] = blocks.astype(BF16).reshape(
                SOURCES, BLOCK, NARROW
            )

            def send(k, carry, base=base):
                home = base + lax.rem(chip + k, SOURCES)

                @pl.when(stays(u, home))
                def _():
                    return_stay(u).start()

                @pl.when(jnp.logical_not(stays(u, home)))
                def _():
                    return_copy(u, home).start()

                return carry

            lax.fori_loop(0, SOURCES, send, 0)

    def out_copy(m, to):
        return pltpu.make_async_remote_copy(
            h_out.at[m, :, to * 896:(to + 1) * 896], out.at[m], h_sent, out_sem.at[m],
            device_id=(to, place), device_id_type=MESH,
        )

    def out_stay(m):
        return pltpu.make_async_copy(
            h_out.at[m, :, 3 * 896:4 * 896], out.at[m], out_sem.at[m]
        )

    def combine(m):
        for half in range(2):
            def arrive(k, carry, half=half):
                pltpu.make_async_copy(
                    came.at[m, half, k], came.at[m, half, k], ret_sem.at[m, half, k]
                ).wait()
                return carry

            lax.fori_loop(0, CHIPS, arrive, 0)
            answered = came[m, half].reshape(CHIPS * BLOCK, NARROW)
            slot = lax.rem(m, 2)
            added = jnp.dot(weight_hi[slot], answered, preferred_element_type=F32) + jnp.dot(
                weight_lo[slot], answered, preferred_element_type=F32
            )
            for k in range(PIECES):
                at = slice(half * HALF + k * NARROW, half * HALF + (k + 1) * NARROW)
                h_out[m, :, at] = (
                    hid[m, :, at].astype(F32) + added[k * tokens:(k + 1) * tokens]
                ).astype(BF16)

            @pl.when(section < sections - 1)
            def _():
                relay_copy(m, half).start()

            @pl.when(section == sections - 1)
            def _():
                for to in range(2 * half, min(2 * half + 2, sections - 1)):
                    out_copy(m, to).start()
                if half == 1:
                    out_stay(m).start()

    def step(t, carry):
        u = t - AHEAD

        @pl.when(t == AHEAD)
        def _():
            for copy in weight_copies:
                copy.wait()
            swap_copy.wait_recv()

        @pl.when((t >= AHEAD) & (t < units + AHEAD))
        def _():
            compute(jnp.maximum(u, 0))

        @pl.when((lax.rem(t, 2) == core) & (t < units))
        def _():
            dispatch(t // 2)

        @pl.when((t >= AHEAD + BEHIND) & (lax.rem(t + 8 - AHEAD - BEHIND, 2) == core))
        def _():
            combine((jnp.maximum(t, AHEAD + BEHIND) - AHEAD - BEHIND) // 2)

        return carry

    lax.fori_loop(0, units + AHEAD + BEHIND, step, 0)

    def drain(m, carry):
        def drain_dispatch(step, inner):
            to = lax.rem(chip + step, CHIPS)
            dispatch_copy(m, to // 2, to, chip).wait_send()
            return inner

        lax.fori_loop(1, CHIPS, drain_dispatch, 0)

        @pl.when(side != core)
        def _():
            dispatch_copy(m, chip // 2, chip, chip).wait_send()

        for half in range(2):
            u = 2 * m + half
            for part in range(2):
                between_copy(u, part).wait_send()

            def drain_forward(k, inner, u=u):
                forward_copy(u, core * SOURCES + k).wait_send()
                return inner

            lax.fori_loop(0, SOURCES, drain_forward, 0)

            def drain_return(home, inner, u=u):
                @pl.when(jnp.logical_not(stays(u, home)))
                def _():
                    return_copy(u, home).wait_send()

                return inner

            lax.fori_loop(0, CHIPS, drain_return, 0)

        @pl.when(section < sections - 1)
        def _():
            for half in range(2):
                relay_copy(m, half).wait_send()

        @pl.when(section == sections - 1)
        def _():
            for to in range(sections - 1):
                out_copy(m, to).wait_send()

        out_stay(m).wait()
        return carry

    swap_copy.wait_send()
    lax.fori_loop(0, micros, drain, 0)


def on_device(inputs, routes, norm_gain, router, w_gate, w_up, w_down):
    micros, tokens, features = inputs.shape
    units = 2 * micros
    hidden_units = w_gate.shape[2]
    vmem = pl.BlockSpec(memory_space=pltpu.VMEM)
    anywhere = pl.BlockSpec(memory_space=pl.ANY)
    dma = pltpu.SemaphoreType.DMA
    return pl.pallas_call(
        kernel,
        out_shape=jax.ShapeDtypeStruct((micros, tokens, features // 4), BF16),
        in_specs=[anywhere, vmem, vmem, vmem] + [anywhere] * 3,
        out_specs=vmem,
        scratch_shapes=[
            pltpu.VMEM((hidden_units, features), BF16),
            pltpu.VMEM((hidden_units, features), BF16),
            pltpu.VMEM((2, hidden_units, HALF), BF16),
            pltpu.VMEM((PIECES * PACKED, SOURCES * BLOCK), BF16),
            pltpu.VMEM((SOURCES * BLOCK, PIECES * PACKED), BF16),
            pltpu.VMEM((micros, tokens, features), BF16),
            pltpu.VMEM((8 * BLOCK, PIECES * tokens), BF16),
            pltpu.VMEM((micros, 8 * BLOCK, WIDE), BF16),
            pltpu.VMEM((units, CHIPS, BLOCK, WIDE), BF16),
            pltpu.VMEM((2 * PACKED, features), BF16),
            pltpu.VMEM((units, 2 * PACKED, hidden_units), BF16),
            pltpu.VMEM((units, 2 * PACKED, hidden_units), BF16),
            pltpu.VMEM((2 * PACKED, HALF), F32),
            pltpu.VMEM((2, PIECES * PACKED, NARROW), BF16),
            pltpu.VMEM((units, CHIPS, BLOCK, NARROW), BF16),
            pltpu.VMEM((micros, 2, CHIPS, BLOCK, NARROW), BF16),
            pltpu.VMEM((2, PIECES * tokens, CHIPS * BLOCK), BF16),
            pltpu.VMEM((2, PIECES * tokens, CHIPS * BLOCK), BF16),
            pltpu.VMEM((micros, tokens, features), BF16),
            dma((4,)),
            dma((micros,)),
            dma((units, CHIPS)),
            dma((units,)),
            dma((micros, 2, CHIPS)),
            dma((micros,)),
            dma, dma, dma, dma, dma, dma,
        ],
        compiler_params=pltpu.CompilerParams(
            collective_id=0, has_side_effects=True, vmem_limit_bytes=60 * 2**20
        ),
        name="moe_relay",
    )(
        inputs, jnp.swapaxes(routes[0], 1, 2), norm_gain, router[0].T, w_gate[0].T, w_up[0].T,
        w_down[0],
    )


def solution(mesh):
    return jax.shard_map(
        on_device,
        mesh=mesh,
        in_specs=(
            P(None, "expert", None),
            P("section", None, "expert", None),
            P("section", None),
            P("section", None, None),
            P("section", None, "expert"),
            P("section", None, "expert"),
            P("section", "expert", None),
        ),
        out_specs=P(None, "expert", "section"),
        check_vma=False,
    )
```

```python
import jax
import jax.numpy as jnp
from jax import lax
from jax.experimental import pallas as pl
from jax.experimental.pallas import tpu as pltpu
from jax.sharding import PartitionSpec as P

EPSILON = 1e-06
MESH = pl.DeviceIdType.MESH
F32 = jnp.float32
BF16 = jnp.bfloat16

CAP = 9
HALF = 1792
PIECES = 7
NARROW = 256
BLOCK = 64
SOURCES = 8
PACKED = 80
CHIPS = 16
GROUP = 4
SLICE = 896
LANES = 128
STEPS = [
    (2, 2), (2, 1), (1, 2), (2, 3), (3, 2), (2, 0), (0, 2), (1, 1), (3, 3), (1, 3), (3, 1),
    (1, 0), (0, 1), (3, 0), (0, 3),
]


def fill_selection(sel, unsel):
    down = lax.broadcasted_iota(jnp.int32, (PIECES * PACKED, 1), 0)
    piece, rest = down // PACKED, lax.rem(down, PACKED)
    source, slot = rest // CAP, lax.rem(rest, CAP)
    taken = jnp.where(rest < SOURCES * CAP, source * BLOCK + piece * CAP + slot, -1)
    sel[...] = jnp.where(
        lax.broadcasted_iota(jnp.int32, sel.shape, 1) == taken, 1.0, 0.0
    ).astype(BF16)
    down = lax.broadcasted_iota(jnp.int32, (SOURCES * BLOCK, 1), 0)
    source, rest = down // BLOCK, lax.rem(down, BLOCK)
    piece, slot = rest // CAP, lax.rem(rest, CAP)
    taken = jnp.where(piece < PIECES, piece * PACKED + source * CAP + slot, -1)
    unsel[...] = jnp.where(
        lax.broadcasted_iota(jnp.int32, unsel.shape, 1) == taken, 1.0, 0.0
    ).astype(BF16)


def dot(rows, columns):
    return jnp.dot(rows, columns, preferred_element_type=F32)


def dot_nt(rows, columns):
    return lax.dot_general(
        rows, columns, (((1,), (1,)), ((), ())), preferred_element_type=F32
    )


def kernel(
    inputs, routes, gain, router, gate_in, up_in, down_in,
    out,
    w_gate, w_up, w_down, sel, unsel, routes_other, hid, square_first, square_out, squares,
    placing, d_out, held, packed, mid_out, mid_in, partial, answers, ret_out, came,
    diff_out, diff_in, weight_hi, weight_lo, h_out,
    w_sem, r_sem, h_sem, q_sem, d_sem, f_sem, mid_sem, ret_sem, diff_sem, out_sem,
    swap_sent, route_sent, input_sent, first_sent, d_sent, f_sent, mid_sent, ret_sent,
    diff_sent, h_sent, q_sent,
):
    micros, tokens, _ = inputs.shape
    units = 2 * micros
    section = lax.axis_index("section")
    place = lax.axis_index("expert")
    sections = 4
    core = lax.rem(place, 2)
    chip = place // 2
    x, y = chip // 4, lax.rem(chip, 4)
    sibling = (section, chip * 2 + (1 - core))
    onward = lax.rem(section + 1, sections)

    def remote(src, dst, sent, arrived, device):
        return pltpu.make_async_remote_copy(
            src, dst, sent, arrived, device_id=device, device_id_type=MESH
        )

    def landing(ref, arrived):
        return pltpu.make_async_copy(ref, ref, arrived)

    def columns_of(half):
        return pl.ds(pl.multiple_of(half * HALF, HALF), HALF)

    mine, others = columns_of(core), columns_of(1 - core)
    around = [(lax.rem(x + dx, 4) * 4 + lax.rem(y + dy, 4)) for dx, dy in STEPS]

    weight_copies = [
        pltpu.make_async_copy(gate_in.at[:, mine], w_gate.at[0], w_sem.at[0]),
        pltpu.make_async_copy(up_in.at[:, mine], w_up.at[0], w_sem.at[1]),
        pltpu.make_async_copy(gate_in.at[:, others], w_gate.at[1], w_sem.at[2]),
        pltpu.make_async_copy(up_in.at[:, others], w_up.at[1], w_sem.at[3]),
        pltpu.make_async_copy(down_in.at[:, mine], w_down.at[0], w_sem.at[4]),
    ]
    swap_copy = remote(down_in.at[:, others], w_down.at[1], swap_sent, w_sem.at[5], sibling)
    route_copy = remote(routes, routes_other, route_sent, r_sem, sibling)

    def input_stay(m):
        u = 2 * m + core
        return pltpu.make_async_copy(inputs.at[m, :, mine], hid.at[u], h_sem.at[u])

    def input_copy(m):
        u = 2 * m + core
        return remote(inputs.at[m, :, others], hid.at[u], input_sent, h_sem.at[u], sibling)

    @pl.when(section == 0)
    def _():
        for m in range(micros):
            input_stay(m).start()

    barrier = pltpu.get_barrier_semaphore()

    def greet(device):
        pl.semaphore_signal(barrier, inc=1, device_id=device, device_id_type=MESH)

    greet(sibling)
    for to in around:
        greet((section, to * 2 + core))
    for step in range(1, sections):
        for half in range(2):
            greet((lax.rem(section + step, sections), chip * 2 + half))
    for copy in weight_copies:
        copy.start()
    fill_selection(sel, unsel)
    pl.semaphore_wait(barrier, 1 + len(STEPS) + 2 * (sections - 1))
    route_copy.start()

    def sum_squares(values):
        total = jnp.sum(values * values, axis=-1, keepdims=True)
        return jnp.broadcast_to(total, (tokens, LANES))

    def first_stay(u):
        return pltpu.make_async_copy(
            square_first.at[u], squares.at[u, core], q_sem.at[u, core]
        )

    def first_copy(u):
        return remote(
            square_first.at[u], squares.at[u, core], first_sent, q_sem.at[u, core], sibling
        )

    @pl.when(section == 0)
    def _():
        for m in range(micros):
            input_copy(m).start()

        def first(u, carry):
            landing(hid.at[u], h_sem.at[u]).wait()
            square_first[u] = sum_squares(hid[u].astype(F32))
            first_copy(u).start()
            first_stay(u).start()
            return carry

        lax.fori_loop(0, units, first, 0)

    swap_copy.start()
    route_copy.wait_recv()

    def total(condition, axis):
        return jnp.sum(jnp.where(condition, 1, 0), axis=axis, keepdims=True)

    def grids():
        width = PIECES * tokens
        up_down = lax.broadcasted_iota(jnp.int32, (tokens, width), 0)
        left_right = lax.broadcasted_iota(jnp.int32, (tokens, width), 1)
        return up_down, left_right, lax.rem(left_right, tokens)

    def choices(u):
        up_down, left_right, token_of = grids()
        here = lax.rem(u, 2) == core
        chosen = jnp.where(here, routes[u // 2], routes_other[u // 2])
        square = up_down[:, :tokens] == left_right[:, :tokens]
        first = jnp.sum(jnp.where(square, chosen[0:1], 0), axis=1, keepdims=True)
        second = jnp.sum(jnp.where(square, chosen[1:2], 0), axis=1, keepdims=True)
        repeat = up_down == token_of
        first_row = jnp.sum(jnp.where(repeat, first, 0), axis=0, keepdims=True)
        second_row = jnp.sum(jnp.where(repeat, second, 0), axis=0, keepdims=True)
        return first, second, first_row, second_row

    def dispatch_copy(u, to):
        return remote(
            d_out.at[u, pl.ds(pl.multiple_of(to // 2 * BLOCK, BLOCK), BLOCK)],
            held.at[u, core, chip], d_sent, d_sem.at[u, chip], (section, to * 2 + core),
        )

    def dispatch_stay(u):
        return pltpu.make_async_copy(
            d_out.at[u, pl.ds(pl.multiple_of(chip // 2 * BLOCK, BLOCK), BLOCK)],
            held.at[u, core, chip], d_sem.at[u, chip],
        )

    def diff_copy(u):
        return remote(diff_out.at[u], diff_in.at[u], diff_sent, diff_sem.at[u], sibling)

    def dispatch(u):
        first, second, first_row, second_row = choices(u)
        up_down, left_right, token_of = grids()
        earlier = up_down < token_of
        slot_first = total((first == first_row) & earlier, 0)
        slot_second = total(first == second_row, 0) + total((second == second_row) & earlier, 0)
        width = PIECES * tokens
        piece_row = lax.broadcasted_iota(jnp.int32, (1, width), 1) // tokens * CAP
        target_first = first_row * BLOCK + piece_row + slot_first
        target_second = second_row * BLOCK + piece_row + slot_second
        rows = lax.broadcasted_iota(jnp.int32, (8 * BLOCK, width), 0)
        placing[...] = jnp.where(
            (rows == target_first) | (rows == target_second), 1.0, 0.0
        ).astype(BF16)

        @pl.when(section > 0)
        def _():
            landing(hid.at[u], h_sem.at[u]).wait()

        for half in range(2):
            landing(squares.at[u, half], q_sem.at[u, half]).wait()
        meansq = (squares[u, 0, :, 0:1] + squares[u, 1, :, 0:1]) * (1.0 / (2 * HALF))
        normed = (
            hid[u].astype(F32) * lax.rsqrt(meansq + EPSILON) * gain[:, mine].astype(F32)
        ).astype(BF16)
        stacked = jnp.concatenate(
            [normed[:, k * NARROW:(k + 1) * NARROW] for k in range(PIECES)], axis=0
        )
        d_out[u] = dot(placing[...], stacked).astype(BF16)
        for to in around:
            dispatch_copy(u, to).start()
        dispatch_stay(u).start()

        logits = dot_nt(normed, router[:, mine])
        expert_range = lax.broadcasted_iota(jnp.int32, logits.shape, 1)
        sign = jnp.where(first == expert_range, 1.0, 0.0) - jnp.where(
            second == expert_range, 1.0, 0.0
        )
        diff_out[u] = jnp.broadcast_to(
            jnp.sum(sign * logits, axis=1, keepdims=True), (tokens, LANES)
        )
        diff_copy(u).start()

    def weigh(u):
        first, second, first_row, second_row = choices(u)
        up_down, left_right, _ = grids()
        before = (left_right < up_down) & (left_right < tokens)
        own_first = total((first == first_row) & before, 1)
        own_second = total((second == first_row) & (left_right < tokens), 1) + total(
            (second == second_row) & before, 1
        )
        at_first = first * BLOCK + own_first
        at_second = second * BLOCK + own_second
        landing(diff_in.at[u], diff_sem.at[u]).wait()
        difference = diff_out[u][:, 0:1] + diff_in[u][:, 0:1]
        first_weight = 1.0 / (1.0 + jnp.exp(-difference))
        second_weight = 1.0 - first_weight
        column = lax.broadcasted_iota(jnp.int32, (tokens, CHIPS * BLOCK), 1)
        column = column // (2 * BLOCK) * BLOCK + lax.rem(column, BLOCK)
        for k in range(PIECES):
            weights = jnp.where(column == at_first + k * CAP, first_weight, 0.0) + jnp.where(
                column == at_second + k * CAP, second_weight, 0.0
            )
            high = weights.astype(BF16)
            weight_hi[k * tokens:(k + 1) * tokens, :] = high
            weight_lo[k * tokens:(k + 1) * tokens, :] = (weights - high.astype(F32)).astype(BF16)

    def forward_copy(u, half, group):
        at = pl.ds(group * GROUP, GROUP)
        return remote(
            held.at[u, half, at], held.at[u, half, at], f_sent, f_sem.at[u, group], sibling
        )

    def pass_on(u):
        for group in range(CHIPS // GROUP):
            for k in range(group * GROUP, (group + 1) * GROUP):
                landing(held.at[u, core, k], d_sem.at[u, k]).wait()
            forward_copy(u, core, group).start()

    def between_copy(u):
        return remote(mid_out.at[u], mid_in.at[u], mid_sent, mid_sem.at[u], sibling)

    def return_copy(u, home):
        return remote(
            ret_out.at[u, home], came.at[u, chip], ret_sent, ret_sem.at[u, chip],
            (section, home * 2 + core),
        )

    def return_stay(u):
        return pltpu.make_async_copy(
            ret_out.at[u, chip], came.at[u, chip], ret_sem.at[u, chip]
        )

    def pack(u, half, slot):
        for group in range(2):
            blocks = held[u, half, group * SOURCES:(group + 1) * SOURCES]
            chosen = dot(sel[...], blocks.reshape(SOURCES * BLOCK, NARROW)).astype(BF16)
            for k in range(PIECES):
                packed[
                    slot, group * PACKED:(group + 1) * PACKED, k * NARROW:(k + 1) * NARROW
                ] = chosen[k * PACKED:(k + 1) * PACKED]

    def compute(u):
        pack(u, core, 0)
        gated = dot_nt(packed[0], w_gate[0])
        upward = dot_nt(packed[0], w_up[0])
        for group in range(CHIPS // GROUP):
            landing(
                held.at[u, 1 - core, pl.ds(group * GROUP, GROUP)], f_sem.at[u, group]
            ).wait()
        pack(u, 1 - core, 1)
        gated = gated + dot_nt(packed[1], w_gate[1])
        upward = upward + dot_nt(packed[1], w_up[1])
        between = (gated / (1.0 + jnp.exp(-gated)) * upward).astype(BF16)
        mid_out[u] = between
        between_copy(u).start()
        partial[...] = dot(between, w_down[0])
        between_copy(u).wait_recv()
        theirs = mid_in[u]
        for k in range(PIECES):
            at = slice(k * NARROW, (k + 1) * NARROW)
            part = (partial[:, at] + dot(theirs, w_down[1, :, at])).astype(BF16)
            answers[0, k * PACKED:(k + 1) * PACKED] = part[:PACKED]
            answers[1, k * PACKED:(k + 1) * PACKED] = part[PACKED:]
        for group in range(2):
            blocks = dot(unsel[...], answers[group]).astype(BF16)
            ret_out[u, group * SOURCES:(group + 1) * SOURCES] = blocks.reshape(
                SOURCES, BLOCK, NARROW
            )
        for home in around:
            return_copy(u, home).start()
        return_stay(u).start()

    def relay_copy(u):
        return remote(h_out.at[u], hid.at[u], h_sent, h_sem.at[u], (onward, place))

    def square_copy(u, half):
        return remote(
            square_out.at[u], squares.at[u, core], q_sent, q_sem.at[u, core],
            (onward, chip * 2 + half),
        )

    def out_copy(u, q):
        return remote(
            h_out.at[u, :, q * SLICE:(q + 1) * SLICE], out.at[u // 2], h_sent,
            out_sem.at[u // 2], (2 * core + q, chip * 2 + lax.rem(u, 2)),
        )

    def out_stay(u):
        return pltpu.make_async_copy(
            h_out.at[u, :, SLICE:2 * SLICE], out.at[u // 2], out_sem.at[u // 2]
        )

    def stays(u):
        return (core == 1) & (lax.rem(u, 2) == core)

    def combine(u):
        def arrive(k, carry):
            landing(came.at[u, k], ret_sem.at[u, k]).wait()
            return carry

        lax.fori_loop(0, CHIPS, arrive, 0)
        answered = came[u].reshape(CHIPS * BLOCK, NARROW)
        added = dot(weight_hi[...], answered) + dot(weight_lo[...], answered)
        for k in range(PIECES):
            at = slice(k * NARROW, (k + 1) * NARROW)
            h_out[u, :, at] = (
                hid[u, :, at].astype(F32) + added[k * tokens:(k + 1) * tokens]
            ).astype(BF16)

        @pl.when(section < sections - 1)
        def _():
            relay_copy(u).start()
            square_out[u] = sum_squares(h_out[u].astype(F32))
            for half in range(2):
                square_copy(u, half).start()

        @pl.when(section == sections - 1)
        def _():
            out_copy(u, 0).start()

            @pl.when(stays(u))
            def _():
                out_stay(u).start()

            @pl.when(jnp.logical_not(stays(u)))
            def _():
                out_copy(u, 1).start()

    def step(t, carry):
        u = jnp.maximum(t - 1, 0)
        working = (t >= 1) & (t <= units)

        @pl.when(working)
        def _():
            pass_on(u)

        @pl.when(t < units)
        def _():
            dispatch(t)

        @pl.when(t == 1)
        def _():
            for copy in weight_copies:
                copy.wait()
            swap_copy.wait_recv()

        @pl.when(working)
        def _():
            compute(u)

        @pl.when(t >= 2)
        def _():
            combine(jnp.maximum(t - 2, 0))

        @pl.when(working)
        def _():
            weigh(u)

        return carry

    lax.fori_loop(0, units + 2, step, 0)

    swap_copy.wait_send()
    route_copy.wait_send()

    @pl.when(section == 0)
    def _():
        for m in range(micros):
            input_copy(m).wait_send()

    def drain(u, carry):
        @pl.when(section == 0)
        def _():
            first_copy(u).wait_send()

        for to in around:
            dispatch_copy(u, to).wait_send()
            return_copy(u, to).wait_send()
        diff_copy(u).wait_send()
        for group in range(CHIPS // GROUP):
            forward_copy(u, core, group).wait_send()
        between_copy(u).wait_send()

        @pl.when(section < sections - 1)
        def _():
            relay_copy(u).wait_send()
            for half in range(2):
                square_copy(u, half).wait_send()

        @pl.when(section == sections - 1)
        def _():
            out_copy(u, 0).wait_send()

            @pl.when(jnp.logical_not(stays(u)))
            def _():
                out_copy(u, 1).wait_send()

        return carry

    lax.fori_loop(0, units, drain, 0)
    for m in range(micros):
        landing(out.at[m], out_sem.at[m]).wait()


def on_device(inputs, routes, norm_gain, router, w_gate, w_up, w_down):
    micros, tokens, features = inputs.shape
    units = 2 * micros
    hidden_units = w_gate.shape[2]
    vmem = pl.BlockSpec(memory_space=pltpu.VMEM)
    anywhere = pl.BlockSpec(memory_space=pl.ANY)
    dma = pltpu.SemaphoreType.DMA

    def bf16(*shape):
        return pltpu.VMEM(shape, BF16)

    def f32(*shape):
        return pltpu.VMEM(shape, F32)

    return pl.pallas_call(
        kernel,
        out_shape=jax.ShapeDtypeStruct((micros, tokens, SLICE), BF16),
        in_specs=[anywhere, vmem, vmem, vmem] + [anywhere] * 3,
        out_specs=vmem,
        scratch_shapes=[
            bf16(2, hidden_units, HALF),
            bf16(2, hidden_units, HALF),
            bf16(2, hidden_units, HALF),
            bf16(PIECES * PACKED, SOURCES * BLOCK),
            bf16(SOURCES * BLOCK, PIECES * PACKED),
            pltpu.VMEM((micros, 2, tokens), jnp.int32),
            bf16(units, tokens, HALF),
            f32(units, tokens, LANES),
            f32(units, tokens, LANES),
            f32(units, 2, tokens, LANES),
            bf16(8 * BLOCK, PIECES * tokens),
            bf16(units, 8 * BLOCK, NARROW),
            bf16(units, 2, CHIPS, BLOCK, NARROW),
            bf16(2, 2 * PACKED, HALF),
            bf16(units, 2 * PACKED, hidden_units),
            bf16(units, 2 * PACKED, hidden_units),
            f32(2 * PACKED, HALF),
            bf16(2, PIECES * PACKED, NARROW),
            bf16(units, CHIPS, BLOCK, NARROW),
            bf16(units, CHIPS, BLOCK, NARROW),
            f32(units, tokens, LANES),
            f32(units, tokens, LANES),
            bf16(PIECES * tokens, CHIPS * BLOCK),
            bf16(PIECES * tokens, CHIPS * BLOCK),
            bf16(units, tokens, HALF),
            dma((6,)),
            dma,
            dma((units,)),
            dma((units, 2)),
            dma((units, CHIPS)),
            dma((units, CHIPS // GROUP)),
            dma((units,)),
            dma((units, CHIPS)),
            dma((units,)),
            dma((micros,)),
        ] + [dma] * 11,
        compiler_params=pltpu.CompilerParams(
            collective_id=0, has_side_effects=True, vmem_limit_bytes=60 * 2**20
        ),
        name="moe_relay",
    )(
        inputs, jnp.swapaxes(routes[0], 1, 2), norm_gain, router[0].T, w_gate[0].T, w_up[0].T,
        w_down[0],
    )


def solution(mesh):
    return jax.shard_map(
        on_device,
        mesh=mesh,
        in_specs=(
            P(None, "expert", None),
            P("section", None, "expert", None),
            P("section", None),
            P("section", None, None),
            P("section", None, "expert"),
            P("section", None, "expert"),
            P("section", "expert", None),
        ),
        out_specs=P(None, "expert", "section"),
        check_vma=False,
    )
```

```python
import jax
import jax.numpy as jnp
from jax import lax
from jax.experimental import pallas as pl
from jax.experimental.pallas import tpu as pltpu
from jax.sharding import PartitionSpec as P

EPSILON = 1e-06
MESH = pl.DeviceIdType.MESH
F32 = jnp.float32
BF16 = jnp.bfloat16

CAP = 9
HALF = 1792
PIECES = 7
NARROW = 256
BLOCK = 64
SOURCES = 8
PACKED = 80
CHIPS = 16
GROUP = 4
SLICE = 896
LANES = 128
STEPS = [
    (2, 2), (2, 1), (1, 2), (2, 3), (3, 2), (2, 0), (0, 2), (1, 1), (3, 3), (1, 3), (3, 1),
    (1, 0), (0, 1), (3, 0), (0, 3),
]


def fill_selection(sel, unsel):
    down = lax.broadcasted_iota(jnp.int32, (PIECES * PACKED, 1), 0)
    piece, rest = down // PACKED, lax.rem(down, PACKED)
    source, slot = rest // CAP, lax.rem(rest, CAP)
    taken = jnp.where(rest < SOURCES * CAP, source * BLOCK + piece * CAP + slot, -1)
    sel[...] = jnp.where(
        lax.broadcasted_iota(jnp.int32, sel.shape, 1) == taken, 1.0, 0.0
    ).astype(BF16)
    down = lax.broadcasted_iota(jnp.int32, (SOURCES * BLOCK, 1), 0)
    source, rest = down // BLOCK, lax.rem(down, BLOCK)
    piece, slot = rest // CAP, lax.rem(rest, CAP)
    taken = jnp.where(piece < PIECES, piece * PACKED + source * CAP + slot, -1)
    unsel[...] = jnp.where(
        lax.broadcasted_iota(jnp.int32, unsel.shape, 1) == taken, 1.0, 0.0
    ).astype(BF16)


def dot(rows, columns):
    return jnp.dot(rows, columns, preferred_element_type=F32)


def dot_nt(rows, columns):
    return lax.dot_general(
        rows, columns, (((1,), (1,)), ((), ())), preferred_element_type=F32
    )


def kernel(
    inputs, routes, gain, router, gate_in, up_in, down_in,
    out,
    w_gate, w_up, w_gate_turned, w_up_turned, w_down, sel, unsel, routes_other, hid, square_first, square_out, squares,
    placing, d_out, held, packed, mid_out, mid_in, partial, answers, ret_out, came,
    diff_out, diff_in, weight_hi, weight_lo, h_out,
    w_sem, r_sem, h_sem, q_sem, d_sem, f_sem, mid_sem, ret_sem, diff_sem, out_sem,
    swap_sent, route_sent, input_sent, first_sent, d_sent, f_sent, mid_sent, ret_sent,
    diff_sent, h_sent, q_sent,
):
    micros, tokens, _ = inputs.shape
    units = 2 * micros
    section = lax.axis_index("section")
    place = lax.axis_index("expert")
    sections = 4
    core = lax.rem(place, 2)
    chip = place // 2
    x, y = chip // 4, lax.rem(chip, 4)
    sibling = (section, chip * 2 + (1 - core))
    onward = lax.rem(section + 1, sections)

    def remote(src, dst, sent, arrived, device):
        return pltpu.make_async_remote_copy(
            src, dst, sent, arrived, device_id=device, device_id_type=MESH
        )

    def landing(ref, arrived):
        return pltpu.make_async_copy(ref, ref, arrived)

    def columns_of(half):
        return pl.ds(pl.multiple_of(half * HALF, HALF), HALF)

    mine, others = columns_of(core), columns_of(1 - core)
    around = [(lax.rem(x + dx, 4) * 4 + lax.rem(y + dy, 4)) for dx, dy in STEPS]

    weight_copies = [
        pltpu.make_async_copy(gate_in.at[:, mine], w_gate.at[0], w_sem.at[0]),
        pltpu.make_async_copy(up_in.at[:, mine], w_up.at[0], w_sem.at[1]),
        pltpu.make_async_copy(gate_in.at[:, others], w_gate.at[1], w_sem.at[2]),
        pltpu.make_async_copy(up_in.at[:, others], w_up.at[1], w_sem.at[3]),
        pltpu.make_async_copy(down_in.at[:, mine], w_down.at[0], w_sem.at[4]),
    ]
    swap_copy = remote(down_in.at[:, others], w_down.at[1], swap_sent, w_sem.at[5], sibling)
    route_copy = remote(routes, routes_other, route_sent, r_sem, sibling)

    def input_stay(m):
        u = 2 * m + core
        return pltpu.make_async_copy(inputs.at[m, :, mine], hid.at[u], h_sem.at[u])

    def input_copy(m):
        u = 2 * m + core
        return remote(inputs.at[m, :, others], hid.at[u], input_sent, h_sem.at[u], sibling)

    @pl.when(section == 0)
    def _():
        for m in range(micros):
            input_stay(m).start()

    barrier = pltpu.get_barrier_semaphore()

    def greet(device):
        pl.semaphore_signal(barrier, inc=1, device_id=device, device_id_type=MESH)

    greet(sibling)
    for to in around:
        greet((section, to * 2 + core))
    for step in range(1, sections):
        for half in range(2):
            greet((lax.rem(section + step, sections), chip * 2 + half))
    for copy in weight_copies:
        copy.start()
    fill_selection(sel, unsel)
    pl.semaphore_wait(barrier, 1 + len(STEPS) + 2 * (sections - 1))
    route_copy.start()

    def sum_squares(values):
        total = jnp.sum(values * values, axis=-1, keepdims=True)
        return jnp.broadcast_to(total, (tokens, LANES))

    def first_stay(u):
        return pltpu.make_async_copy(
            square_first.at[u], squares.at[u, core], q_sem.at[u, core]
        )

    def first_copy(u):
        return remote(
            square_first.at[u], squares.at[u, core], first_sent, q_sem.at[u, core], sibling
        )

    @pl.when(section == 0)
    def _():
        for m in range(micros):
            input_copy(m).start()

        def first(u, carry):
            landing(hid.at[u], h_sem.at[u]).wait()
            square_first[u] = sum_squares(hid[u].astype(F32))
            first_copy(u).start()
            first_stay(u).start()
            return carry

        lax.fori_loop(0, units, first, 0)

    swap_copy.start()
    route_copy.wait_recv()

    def total(condition, axis):
        return jnp.sum(jnp.where(condition, 1, 0), axis=axis, keepdims=True)

    def grids():
        width = PIECES * tokens
        up_down = lax.broadcasted_iota(jnp.int32, (tokens, width), 0)
        left_right = lax.broadcasted_iota(jnp.int32, (tokens, width), 1)
        return up_down, left_right, lax.rem(left_right, tokens)

    def choices(u):
        up_down, left_right, token_of = grids()
        here = lax.rem(u, 2) == core
        chosen = jnp.where(here, routes[u // 2], routes_other[u // 2])
        square = up_down[:, :tokens] == left_right[:, :tokens]
        first = jnp.sum(jnp.where(square, chosen[0:1], 0), axis=1, keepdims=True)
        second = jnp.sum(jnp.where(square, chosen[1:2], 0), axis=1, keepdims=True)
        repeat = up_down == token_of
        first_row = jnp.sum(jnp.where(repeat, first, 0), axis=0, keepdims=True)
        second_row = jnp.sum(jnp.where(repeat, second, 0), axis=0, keepdims=True)
        return first, second, first_row, second_row

    def dispatch_copy(u, to):
        return remote(
            d_out.at[u, pl.ds(pl.multiple_of(to // 2 * BLOCK, BLOCK), BLOCK)],
            held.at[u, core, chip], d_sent, d_sem.at[u, chip], (section, to * 2 + core),
        )

    def dispatch_stay(u):
        return pltpu.make_async_copy(
            d_out.at[u, pl.ds(pl.multiple_of(chip // 2 * BLOCK, BLOCK), BLOCK)],
            held.at[u, core, chip], d_sem.at[u, chip],
        )

    def diff_copy(u):
        return remote(diff_out.at[u], diff_in.at[u], diff_sent, diff_sem.at[u], sibling)

    def dispatch(u):
        first, second, first_row, second_row = choices(u)
        up_down, left_right, token_of = grids()
        earlier = up_down < token_of
        slot_first = total((first == first_row) & earlier, 0)
        slot_second = total(first == second_row, 0) + total((second == second_row) & earlier, 0)
        width = PIECES * tokens
        piece_row = lax.broadcasted_iota(jnp.int32, (1, width), 1) // tokens * CAP
        target_first = first_row * BLOCK + piece_row + slot_first
        target_second = second_row * BLOCK + piece_row + slot_second
        rows = lax.broadcasted_iota(jnp.int32, (8 * BLOCK, width), 0)
        placing[...] = jnp.where(
            (rows == target_first) | (rows == target_second), 1.0, 0.0
        ).astype(BF16)

        @pl.when(section > 0)
        def _():
            landing(hid.at[u], h_sem.at[u]).wait()

        for half in range(2):
            landing(squares.at[u, half], q_sem.at[u, half]).wait()
        meansq = (squares[u, 0, :, 0:1] + squares[u, 1, :, 0:1]) * (1.0 / (2 * HALF))
        normed = (
            hid[u].astype(F32) * lax.rsqrt(meansq + EPSILON) * gain[:, mine].astype(F32)
        ).astype(BF16)
        stacked = jnp.concatenate(
            [normed[:, k * NARROW:(k + 1) * NARROW] for k in range(PIECES)], axis=0
        )
        d_out[u] = dot(placing[...], stacked).astype(BF16)
        for to in around:
            dispatch_copy(u, to).start()
        dispatch_stay(u).start()

        logits = dot_nt(normed, router[:, mine])
        expert_range = lax.broadcasted_iota(jnp.int32, logits.shape, 1)
        sign = jnp.where(first == expert_range, 1.0, 0.0) - jnp.where(
            second == expert_range, 1.0, 0.0
        )
        diff_out[u] = jnp.broadcast_to(
            jnp.sum(sign * logits, axis=1, keepdims=True), (tokens, LANES)
        )
        diff_copy(u).start()

    def weigh(u):
        first, second, first_row, second_row = choices(u)
        up_down, left_right, _ = grids()
        before = (left_right < up_down) & (left_right < tokens)
        own_first = total((first == first_row) & before, 1)
        own_second = total((second == first_row) & (left_right < tokens), 1) + total(
            (second == second_row) & before, 1
        )
        at_first = first * BLOCK + own_first
        at_second = second * BLOCK + own_second
        landing(diff_in.at[u], diff_sem.at[u]).wait()
        difference = diff_out[u][:, 0:1] + diff_in[u][:, 0:1]
        first_weight = 1.0 / (1.0 + jnp.exp(-difference))
        second_weight = 1.0 - first_weight
        column = lax.broadcasted_iota(jnp.int32, (tokens, CHIPS * BLOCK), 1)
        column = column // (2 * BLOCK) * BLOCK + lax.rem(column, BLOCK)
        for k in range(PIECES):
            weights = jnp.where(column == at_first + k * CAP, first_weight, 0.0) + jnp.where(
                column == at_second + k * CAP, second_weight, 0.0
            )
            high = weights.astype(BF16)
            weight_hi[k * tokens:(k + 1) * tokens, :] = high
            weight_lo[k * tokens:(k + 1) * tokens, :] = (weights - high.astype(F32)).astype(BF16)

    def forward_copy(u, half, group):
        at = pl.ds(group * GROUP, GROUP)
        return remote(
            held.at[u, half, at], held.at[u, half, at], f_sent, f_sem.at[u, group], sibling
        )

    def pass_on(u):
        for group in range(CHIPS // GROUP):
            for k in range(group * GROUP, (group + 1) * GROUP):
                landing(held.at[u, core, k], d_sem.at[u, k]).wait()
            forward_copy(u, core, group).start()

    def between_copy(u):
        return remote(mid_out.at[u], mid_in.at[u], mid_sent, mid_sem.at[u], sibling)

    def return_copy(u, home):
        return remote(
            ret_out.at[u, home], came.at[u, chip], ret_sent, ret_sem.at[u, chip],
            (section, home * 2 + core),
        )

    def return_stay(u):
        return pltpu.make_async_copy(
            ret_out.at[u, chip], came.at[u, chip], ret_sem.at[u, chip]
        )

    def pack(u, half, slot):
        for group in range(2):
            blocks = held[u, half, group * SOURCES:(group + 1) * SOURCES]
            chosen = dot(sel[...], blocks.reshape(SOURCES * BLOCK, NARROW)).astype(BF16)
            for k in range(PIECES):
                packed[
                    slot, group * PACKED:(group + 1) * PACKED, k * NARROW:(k + 1) * NARROW
                ] = chosen[k * PACKED:(k + 1) * PACKED]

    def compute(u):
        pack(u, core, 0)
        gated = dot(packed[0], w_gate_turned[0])
        upward = dot(packed[0], w_up_turned[0])
        for group in range(CHIPS // GROUP):
            landing(
                held.at[u, 1 - core, pl.ds(group * GROUP, GROUP)], f_sem.at[u, group]
            ).wait()
        pack(u, 1 - core, 1)
        gated = gated + dot(packed[1], w_gate_turned[1])
        upward = upward + dot(packed[1], w_up_turned[1])
        between = (gated / (1.0 + jnp.exp(-gated)) * upward).astype(BF16)
        mid_out[u] = between
        between_copy(u).start()
        partial[...] = dot(between, w_down[0])
        between_copy(u).wait_recv()
        theirs = mid_in[u]
        for k in range(PIECES):
            at = slice(k * NARROW, (k + 1) * NARROW)
            part = (partial[:, at] + dot(theirs, w_down[1, :, at])).astype(BF16)
            answers[0, k * PACKED:(k + 1) * PACKED] = part[:PACKED]
            answers[1, k * PACKED:(k + 1) * PACKED] = part[PACKED:]
        for group in range(2):
            blocks = dot(unsel[...], answers[group]).astype(BF16)
            ret_out[u, group * SOURCES:(group + 1) * SOURCES] = blocks.reshape(
                SOURCES, BLOCK, NARROW
            )
        for home in around:
            return_copy(u, home).start()
        return_stay(u).start()

    def relay_copy(u):
        return remote(h_out.at[u], hid.at[u], h_sent, h_sem.at[u], (onward, place))

    def square_copy(u, half):
        return remote(
            square_out.at[u], squares.at[u, core], q_sent, q_sem.at[u, core],
            (onward, chip * 2 + half),
        )

    def out_copy(u, q):
        return remote(
            h_out.at[u, :, q * SLICE:(q + 1) * SLICE], out.at[u // 2], h_sent,
            out_sem.at[u // 2], (2 * core + q, chip * 2 + lax.rem(u, 2)),
        )

    def out_stay(u):
        return pltpu.make_async_copy(
            h_out.at[u, :, SLICE:2 * SLICE], out.at[u // 2], out_sem.at[u // 2]
        )

    def stays(u):
        return (core == 1) & (lax.rem(u, 2) == core)

    def combine(u):
        def arrive(k, carry):
            landing(came.at[u, k], ret_sem.at[u, k]).wait()
            return carry

        lax.fori_loop(0, CHIPS, arrive, 0)
        answered = came[u].reshape(CHIPS * BLOCK, NARROW)
        added = dot(weight_hi[...], answered) + dot(weight_lo[...], answered)
        for k in range(PIECES):
            at = slice(k * NARROW, (k + 1) * NARROW)
            h_out[u, :, at] = (
                hid[u, :, at].astype(F32) + added[k * tokens:(k + 1) * tokens]
            ).astype(BF16)

        @pl.when(section < sections - 1)
        def _():
            relay_copy(u).start()
            square_out[u] = sum_squares(h_out[u].astype(F32))
            for half in range(2):
                square_copy(u, half).start()

        @pl.when(section == sections - 1)
        def _():
            out_copy(u, 0).start()

            @pl.when(stays(u))
            def _():
                out_stay(u).start()

            @pl.when(jnp.logical_not(stays(u)))
            def _():
                out_copy(u, 1).start()

    def turn():
        for copy in weight_copies:
            copy.wait()

        def turn_columns(k, carry):
            at = pl.ds(pl.multiple_of(k * LANES, LANES), LANES)
            for half in range(2):
                w_gate_turned[half, at, :] = w_gate[half, :, at].T
                w_up_turned[half, at, :] = w_up[half, :, at].T
            return carry

        lax.fori_loop(0, HALF // LANES, turn_columns, 0)

    @pl.when(section > 0)
    def _():
        turn()

    def step(t, carry):
        u = jnp.maximum(t - 1, 0)
        working = (t >= 1) & (t <= units)

        @pl.when(working)
        def _():
            pass_on(u)

        @pl.when(t < units)
        def _():
            dispatch(t)

        @pl.when((t == 0) & (section == 0))
        def _():
            turn()

        @pl.when(t == 1)
        def _():
            swap_copy.wait_recv()

        @pl.when(working)
        def _():
            compute(u)

        @pl.when(t >= 2)
        def _():
            combine(jnp.maximum(t - 2, 0))

        @pl.when(working)
        def _():
            weigh(u)

        return carry

    lax.fori_loop(0, units + 2, step, 0)

    swap_copy.wait_send()
    route_copy.wait_send()

    @pl.when(section == 0)
    def _():
        for m in range(micros):
            input_copy(m).wait_send()

    def drain(u, carry):
        @pl.when(section == 0)
        def _():
            first_copy(u).wait_send()

        for to in around:
            dispatch_copy(u, to).wait_send()
            return_copy(u, to).wait_send()
        diff_copy(u).wait_send()
        for group in range(CHIPS // GROUP):
            forward_copy(u, core, group).wait_send()
        between_copy(u).wait_send()

        @pl.when(section < sections - 1)
        def _():
            relay_copy(u).wait_send()
            for half in range(2):
                square_copy(u, half).wait_send()

        @pl.when(section == sections - 1)
        def _():
            out_copy(u, 0).wait_send()

            @pl.when(jnp.logical_not(stays(u)))
            def _():
                out_copy(u, 1).wait_send()

        return carry

    lax.fori_loop(0, units, drain, 0)
    for m in range(micros):
        landing(out.at[m], out_sem.at[m]).wait()


def on_device(inputs, routes, norm_gain, router, w_gate, w_up, w_down):
    micros, tokens, features = inputs.shape
    units = 2 * micros
    hidden_units = w_gate.shape[2]
    vmem = pl.BlockSpec(memory_space=pltpu.VMEM)
    anywhere = pl.BlockSpec(memory_space=pl.ANY)
    dma = pltpu.SemaphoreType.DMA

    def bf16(*shape):
        return pltpu.VMEM(shape, BF16)

    def f32(*shape):
        return pltpu.VMEM(shape, F32)

    return pl.pallas_call(
        kernel,
        out_shape=jax.ShapeDtypeStruct((micros, tokens, SLICE), BF16),
        in_specs=[anywhere, vmem, vmem, vmem] + [anywhere] * 3,
        out_specs=vmem,
        scratch_shapes=[
            bf16(2, hidden_units, HALF),
            bf16(2, hidden_units, HALF),
            bf16(2, HALF, hidden_units),
            bf16(2, HALF, hidden_units),
            bf16(2, hidden_units, HALF),
            bf16(PIECES * PACKED, SOURCES * BLOCK),
            bf16(SOURCES * BLOCK, PIECES * PACKED),
            pltpu.VMEM((micros, 2, tokens), jnp.int32),
            bf16(units, tokens, HALF),
            f32(units, tokens, LANES),
            f32(units, tokens, LANES),
            f32(units, 2, tokens, LANES),
            bf16(8 * BLOCK, PIECES * tokens),
            bf16(units, 8 * BLOCK, NARROW),
            bf16(units, 2, CHIPS, BLOCK, NARROW),
            bf16(2, 2 * PACKED, HALF),
            bf16(units, 2 * PACKED, hidden_units),
            bf16(units, 2 * PACKED, hidden_units),
            f32(2 * PACKED, HALF),
            bf16(2, PIECES * PACKED, NARROW),
            bf16(units, CHIPS, BLOCK, NARROW),
            bf16(units, CHIPS, BLOCK, NARROW),
            f32(units, tokens, LANES),
            f32(units, tokens, LANES),
            bf16(PIECES * tokens, CHIPS * BLOCK),
            bf16(PIECES * tokens, CHIPS * BLOCK),
            bf16(units, tokens, HALF),
            dma((6,)),
            dma,
            dma((units,)),
            dma((units, 2)),
            dma((units, CHIPS)),
            dma((units, CHIPS // GROUP)),
            dma((units,)),
            dma((units, CHIPS)),
            dma((units,)),
            dma((micros,)),
        ] + [dma] * 11,
        compiler_params=pltpu.CompilerParams(
            collective_id=0, has_side_effects=True, vmem_limit_bytes=60 * 2**20
        ),
        name="moe_relay",
    )(
        inputs, jnp.swapaxes(routes[0], 1, 2), norm_gain, router[0].T, w_gate[0].T, w_up[0].T,
        w_down[0],
    )


def solution(mesh):
    return jax.shard_map(
        on_device,
        mesh=mesh,
        in_specs=(
            P(None, "expert", None),
            P("section", None, "expert", None),
            P("section", None),
            P("section", None, None),
            P("section", None, "expert"),
            P("section", None, "expert"),
            P("section", "expert", None),
        ),
        out_specs=P(None, "expert", "section"),
        check_vma=False,
    )
```

```python
import jax
import jax.numpy as jnp
from jax import lax
from jax.experimental import pallas as pl
from jax.experimental.pallas import tpu as pltpu
from jax.sharding import PartitionSpec as P

EPSILON = 1e-06
MESH = pl.DeviceIdType.MESH
F32 = jnp.float32
BF16 = jnp.bfloat16

CAP = 9
HALF = 1792
PIECES = 7
NARROW = 256
BLOCK = 64
SOURCES = 8
PACKED = 80
CHIPS = 16
GROUP = 4
SLICE = 896
LANES = 128
STEPS = [
    (2, 2), (2, 1), (1, 2), (2, 3), (3, 2), (2, 0), (0, 2), (1, 1), (3, 3), (1, 3), (3, 1),
    (1, 0), (0, 1), (3, 0), (0, 3),
]


def fill_selection(sel, unsel):
    down = lax.broadcasted_iota(jnp.int32, (PIECES * PACKED, 1), 0)
    piece, rest = down // PACKED, lax.rem(down, PACKED)
    source, slot = rest // CAP, lax.rem(rest, CAP)
    taken = jnp.where(rest < SOURCES * CAP, source * BLOCK + piece * CAP + slot, -1)
    sel[...] = jnp.where(
        lax.broadcasted_iota(jnp.int32, sel.shape, 1) == taken, 1.0, 0.0
    ).astype(BF16)
    down = lax.broadcasted_iota(jnp.int32, (SOURCES * BLOCK, 1), 0)
    source, rest = down // BLOCK, lax.rem(down, BLOCK)
    piece, slot = rest // CAP, lax.rem(rest, CAP)
    taken = jnp.where(piece < PIECES, piece * PACKED + source * CAP + slot, -1)
    unsel[...] = jnp.where(
        lax.broadcasted_iota(jnp.int32, unsel.shape, 1) == taken, 1.0, 0.0
    ).astype(BF16)


def dot(rows, columns):
    return jnp.dot(rows, columns, preferred_element_type=F32)


def dot_nt(rows, columns):
    return lax.dot_general(
        rows, columns, (((1,), (1,)), ((), ())), preferred_element_type=F32
    )


def kernel(
    inputs, routes, gain, router, gate_in, up_in, down_in,
    out,
    w_gate, w_up, w_gate_turned, w_up_turned, w_down, sel, unsel, routes_other, hid, square_first, square_out, squares,
    placing, d_out, held, packed, mid_out, mid_in, partial, answers, ret_out, came,
    diff_out, diff_in, weights, h_out,
    w_sem, r_sem, h_sem, q_sem, d_sem, f_sem, mid_sem, ret_sem, diff_sem, out_sem,
    swap_sent, route_sent, input_sent, first_sent, d_sent, f_sent, mid_sent, ret_sent,
    diff_sent, h_sent, q_sent,
):
    micros, tokens, _ = inputs.shape
    units = 2 * micros
    section = lax.axis_index("section")
    place = lax.axis_index("expert")
    sections = 4
    core = lax.rem(place, 2)
    chip = place // 2
    x, y = chip // 4, lax.rem(chip, 4)
    sibling = (section, chip * 2 + (1 - core))
    onward = lax.rem(section + 1, sections)

    def remote(src, dst, sent, arrived, device):
        return pltpu.make_async_remote_copy(
            src, dst, sent, arrived, device_id=device, device_id_type=MESH
        )

    def landing(ref, arrived):
        return pltpu.make_async_copy(ref, ref, arrived)

    def columns_of(half):
        return pl.ds(pl.multiple_of(half * HALF, HALF), HALF)

    mine, others = columns_of(core), columns_of(1 - core)
    around = [(lax.rem(x + dx, 4) * 4 + lax.rem(y + dy, 4)) for dx, dy in STEPS]

    weight_copies = [
        pltpu.make_async_copy(gate_in.at[:, mine], w_gate.at[0], w_sem.at[0]),
        pltpu.make_async_copy(up_in.at[:, mine], w_up.at[0], w_sem.at[1]),
        pltpu.make_async_copy(gate_in.at[:, others], w_gate.at[1], w_sem.at[2]),
        pltpu.make_async_copy(up_in.at[:, others], w_up.at[1], w_sem.at[3]),
        pltpu.make_async_copy(down_in.at[:, mine], w_down.at[0], w_sem.at[4]),
    ]
    swap_copy = remote(down_in.at[:, others], w_down.at[1], swap_sent, w_sem.at[5], sibling)
    route_copy = remote(routes, routes_other, route_sent, r_sem, sibling)

    def input_stay(m):
        u = 2 * m + core
        return pltpu.make_async_copy(inputs.at[m, :, mine], hid.at[u], h_sem.at[u])

    def input_copy(m):
        u = 2 * m + core
        return remote(inputs.at[m, :, others], hid.at[u], input_sent, h_sem.at[u], sibling)

    @pl.when(section == 0)
    def _():
        for m in range(micros):
            input_stay(m).start()

    barrier = pltpu.get_barrier_semaphore()

    def greet(device):
        pl.semaphore_signal(barrier, inc=1, device_id=device, device_id_type=MESH)

    greet(sibling)
    for to in around:
        greet((section, to * 2 + core))
    for step in range(1, sections):
        for half in range(2):
            greet((lax.rem(section + step, sections), chip * 2 + half))
    for copy in weight_copies:
        copy.start()
    fill_selection(sel, unsel)
    pl.semaphore_wait(barrier, 1 + len(STEPS) + 2 * (sections - 1))
    route_copy.start()

    def sum_squares(values):
        total = jnp.sum(values * values, axis=-1, keepdims=True)
        return jnp.broadcast_to(total, (tokens, LANES))

    def first_stay(u):
        return pltpu.make_async_copy(
            square_first.at[u], squares.at[u, core], q_sem.at[u, core]
        )

    def first_copy(u):
        return remote(
            square_first.at[u], squares.at[u, core], first_sent, q_sem.at[u, core], sibling
        )

    @pl.when(section == 0)
    def _():
        for m in range(micros):
            input_copy(m).start()

        def first(u, carry):
            landing(hid.at[u], h_sem.at[u]).wait()
            square_first[u] = sum_squares(hid[u].astype(F32))
            first_copy(u).start()
            first_stay(u).start()
            return carry

        lax.fori_loop(0, units, first, 0)

    swap_copy.start()
    route_copy.wait_recv()

    def total(condition, axis):
        return jnp.sum(jnp.where(condition, 1, 0), axis=axis, keepdims=True)

    def grids():
        width = PIECES * tokens
        up_down = lax.broadcasted_iota(jnp.int32, (tokens, width), 0)
        left_right = lax.broadcasted_iota(jnp.int32, (tokens, width), 1)
        return up_down, left_right, lax.rem(left_right, tokens)

    def choices(u):
        up_down, left_right, token_of = grids()
        here = lax.rem(u, 2) == core
        chosen = jnp.where(here, routes[u // 2], routes_other[u // 2])
        square = up_down[:, :tokens] == left_right[:, :tokens]
        first = jnp.sum(jnp.where(square, chosen[0:1], 0), axis=1, keepdims=True)
        second = jnp.sum(jnp.where(square, chosen[1:2], 0), axis=1, keepdims=True)
        repeat = up_down == token_of
        first_row = jnp.sum(jnp.where(repeat, first, 0), axis=0, keepdims=True)
        second_row = jnp.sum(jnp.where(repeat, second, 0), axis=0, keepdims=True)
        return first, second, first_row, second_row

    def dispatch_copy(u, to):
        return remote(
            d_out.at[u, pl.ds(pl.multiple_of(to // 2 * BLOCK, BLOCK), BLOCK)],
            held.at[u, core, chip], d_sent, d_sem.at[u, chip], (section, to * 2 + core),
        )

    def dispatch_stay(u):
        return pltpu.make_async_copy(
            d_out.at[u, pl.ds(pl.multiple_of(chip // 2 * BLOCK, BLOCK), BLOCK)],
            held.at[u, core, chip], d_sem.at[u, chip],
        )

    def diff_copy(u):
        return remote(diff_out.at[u], diff_in.at[u], diff_sent, diff_sem.at[u], sibling)

    def dispatch(u):
        first, second, first_row, second_row = choices(u)
        up_down, left_right, token_of = grids()
        earlier = up_down < token_of
        slot_first = total((first == first_row) & earlier, 0)
        slot_second = total(first == second_row, 0) + total((second == second_row) & earlier, 0)
        width = PIECES * tokens
        piece_row = lax.broadcasted_iota(jnp.int32, (1, width), 1) // tokens * CAP
        target_first = first_row * BLOCK + piece_row + slot_first
        target_second = second_row * BLOCK + piece_row + slot_second
        rows = lax.broadcasted_iota(jnp.int32, (8 * BLOCK, width), 0)
        placing[...] = jnp.where(
            (rows == target_first) | (rows == target_second), 1.0, 0.0
        ).astype(BF16)

        @pl.when(section > 0)
        def _():
            landing(hid.at[u], h_sem.at[u]).wait()

        for half in range(2):
            landing(squares.at[u, half], q_sem.at[u, half]).wait()
        meansq = (squares[u, 0, :, 0:1] + squares[u, 1, :, 0:1]) * (1.0 / (2 * HALF))
        normed = (
            hid[u].astype(F32) * lax.rsqrt(meansq + EPSILON) * gain[:, mine].astype(F32)
        ).astype(BF16)
        stacked = jnp.concatenate(
            [normed[:, k * NARROW:(k + 1) * NARROW] for k in range(PIECES)], axis=0
        )
        d_out[u] = dot(placing[...], stacked).astype(BF16)
        for to in around:
            dispatch_copy(u, to).start()
        dispatch_stay(u).start()

        logits = dot_nt(normed, router[:, mine])
        expert_range = lax.broadcasted_iota(jnp.int32, logits.shape, 1)
        sign = jnp.where(first == expert_range, 1.0, 0.0) - jnp.where(
            second == expert_range, 1.0, 0.0
        )
        diff_out[u] = jnp.broadcast_to(
            jnp.sum(sign * logits, axis=1, keepdims=True), (tokens, LANES)
        )
        diff_copy(u).start()

    def weigh(u):
        first, second, first_row, second_row = choices(u)
        up_down, left_right, _ = grids()
        before = (left_right < up_down) & (left_right < tokens)
        own_first = total((first == first_row) & before, 1)
        own_second = total((second == first_row) & (left_right < tokens), 1) + total(
            (second == second_row) & before, 1
        )
        at_first = first * BLOCK + own_first
        at_second = second * BLOCK + own_second
        landing(diff_in.at[u], diff_sem.at[u]).wait()
        difference = diff_out[u][:, 0:1] + diff_in[u][:, 0:1]
        first_weight = 1.0 / (1.0 + jnp.exp(-difference))
        second_weight = 1.0 - first_weight
        column = lax.broadcasted_iota(jnp.int32, (tokens, CHIPS * BLOCK), 1)
        column = column // (2 * BLOCK) * BLOCK + lax.rem(column, BLOCK)
        for k in range(PIECES):
            weights[k * tokens:(k + 1) * tokens, :] = jnp.where(
                column == at_first + k * CAP,
                first_weight,
                jnp.where(column == at_second + k * CAP, second_weight, 0.0),
            ).astype(BF16)

    def forward_copy(u, half, group):
        at = pl.ds(group * GROUP, GROUP)
        return remote(
            held.at[u, half, at], held.at[u, half, at], f_sent, f_sem.at[u, group], sibling
        )

    def pass_on(u):
        for group in range(CHIPS // GROUP):
            for k in range(group * GROUP, (group + 1) * GROUP):
                landing(held.at[u, core, k], d_sem.at[u, k]).wait()
            forward_copy(u, core, group).start()

    def between_copy(u):
        return remote(mid_out.at[u], mid_in.at[u], mid_sent, mid_sem.at[u], sibling)

    def return_copy(u, home):
        return remote(
            ret_out.at[u, home], came.at[u, chip], ret_sent, ret_sem.at[u, chip],
            (section, home * 2 + core),
        )

    def return_stay(u):
        return pltpu.make_async_copy(
            ret_out.at[u, chip], came.at[u, chip], ret_sem.at[u, chip]
        )

    def pack(u, half, slot):
        for group in range(2):
            blocks = held[u, half, group * SOURCES:(group + 1) * SOURCES]
            chosen = dot(sel[...], blocks.reshape(SOURCES * BLOCK, NARROW)).astype(BF16)
            for k in range(PIECES):
                packed[
                    slot, group * PACKED:(group + 1) * PACKED, k * NARROW:(k + 1) * NARROW
                ] = chosen[k * PACKED:(k + 1) * PACKED]

    def compute(u):
        pack(u, core, 0)
        gated = dot(packed[0], w_gate_turned[0])
        upward = dot(packed[0], w_up_turned[0])
        for group in range(CHIPS // GROUP):
            landing(
                held.at[u, 1 - core, pl.ds(group * GROUP, GROUP)], f_sem.at[u, group]
            ).wait()
        pack(u, 1 - core, 1)
        gated = gated + dot(packed[1], w_gate_turned[1])
        upward = upward + dot(packed[1], w_up_turned[1])
        between = (gated / (1.0 + jnp.exp(-gated)) * upward).astype(BF16)
        mid_out[u] = between
        between_copy(u).start()
        partial[...] = dot(between, w_down[0])
        between_copy(u).wait_recv()
        theirs = mid_in[u]
        for k in range(PIECES):
            at = slice(k * NARROW, (k + 1) * NARROW)
            part = (partial[:, at] + dot(theirs, w_down[1, :, at])).astype(BF16)
            answers[0, k * PACKED:(k + 1) * PACKED] = part[:PACKED]
            answers[1, k * PACKED:(k + 1) * PACKED] = part[PACKED:]
        for group in range(2):
            blocks = dot(unsel[...], answers[group]).astype(BF16)
            ret_out[u, group * SOURCES:(group + 1) * SOURCES] = blocks.reshape(
                SOURCES, BLOCK, NARROW
            )
        for home in around:
            return_copy(u, home).start()
        return_stay(u).start()

    def relay_copy(u):
        return remote(h_out.at[u], hid.at[u], h_sent, h_sem.at[u], (onward, place))

    def square_copy(u, half):
        return remote(
            square_out.at[u], squares.at[u, core], q_sent, q_sem.at[u, core],
            (onward, chip * 2 + half),
        )

    def out_copy(u, q):
        return remote(
            h_out.at[u, :, q * SLICE:(q + 1) * SLICE], out.at[u // 2], h_sent,
            out_sem.at[u // 2], (2 * core + q, chip * 2 + lax.rem(u, 2)),
        )

    def out_stay(u):
        return pltpu.make_async_copy(
            h_out.at[u, :, SLICE:2 * SLICE], out.at[u // 2], out_sem.at[u // 2]
        )

    def stays(u):
        return (core == 1) & (lax.rem(u, 2) == core)

    def combine(u):
        def arrive(k, carry):
            landing(came.at[u, k], ret_sem.at[u, k]).wait()
            return carry

        lax.fori_loop(0, CHIPS, arrive, 0)
        answered = came[u].reshape(CHIPS * BLOCK, NARROW)
        added = dot(weights[...], answered)
        for k in range(PIECES):
            at = slice(k * NARROW, (k + 1) * NARROW)
            h_out[u, :, at] = (
                hid[u, :, at].astype(F32) + added[k * tokens:(k + 1) * tokens]
            ).astype(BF16)

        @pl.when(section < sections - 1)
        def _():
            relay_copy(u).start()
            square_out[u] = sum_squares(h_out[u].astype(F32))
            for half in range(2):
                square_copy(u, half).start()

        @pl.when(section == sections - 1)
        def _():
            out_copy(u, 0).start()

            @pl.when(stays(u))
            def _():
                out_stay(u).start()

            @pl.when(jnp.logical_not(stays(u)))
            def _():
                out_copy(u, 1).start()

    def turn():
        for copy in weight_copies:
            copy.wait()

        def turn_columns(k, carry):
            at = pl.ds(pl.multiple_of(k * LANES, LANES), LANES)
            for half in range(2):
                w_gate_turned[half, at, :] = w_gate[half, :, at].T
                w_up_turned[half, at, :] = w_up[half, :, at].T
            return carry

        lax.fori_loop(0, HALF // LANES, turn_columns, 0)

    @pl.when(section > 0)
    def _():
        turn()

    def step(t, carry):
        u = jnp.maximum(t - 1, 0)
        working = (t >= 1) & (t <= units)

        @pl.when(working)
        def _():
            pass_on(u)

        @pl.when(t < units)
        def _():
            dispatch(t)

        @pl.when((t == 0) & (section == 0))
        def _():
            turn()

        @pl.when(t == 1)
        def _():
            swap_copy.wait_recv()

        @pl.when(working)
        def _():
            compute(u)

        @pl.when(t >= 2)
        def _():
            combine(jnp.maximum(t - 2, 0))

        @pl.when(working)
        def _():
            weigh(u)

        return carry

    lax.fori_loop(0, units + 2, step, 0)

    swap_copy.wait_send()
    route_copy.wait_send()

    @pl.when(section == 0)
    def _():
        for m in range(micros):
            input_copy(m).wait_send()

    def drain(u, carry):
        @pl.when(section == 0)
        def _():
            first_copy(u).wait_send()

        for to in around:
            dispatch_copy(u, to).wait_send()
            return_copy(u, to).wait_send()
        diff_copy(u).wait_send()
        for group in range(CHIPS // GROUP):
            forward_copy(u, core, group).wait_send()
        between_copy(u).wait_send()

        @pl.when(section < sections - 1)
        def _():
            relay_copy(u).wait_send()
            for half in range(2):
                square_copy(u, half).wait_send()

        @pl.when(section == sections - 1)
        def _():
            out_copy(u, 0).wait_send()

            @pl.when(jnp.logical_not(stays(u)))
            def _():
                out_copy(u, 1).wait_send()

        return carry

    lax.fori_loop(0, units, drain, 0)
    for m in range(micros):
        landing(out.at[m], out_sem.at[m]).wait()


def on_device(inputs, routes, norm_gain, router, w_gate, w_up, w_down):
    micros, tokens, features = inputs.shape
    units = 2 * micros
    hidden_units = w_gate.shape[2]
    vmem = pl.BlockSpec(memory_space=pltpu.VMEM)
    anywhere = pl.BlockSpec(memory_space=pl.ANY)
    dma = pltpu.SemaphoreType.DMA

    def bf16(*shape):
        return pltpu.VMEM(shape, BF16)

    def f32(*shape):
        return pltpu.VMEM(shape, F32)

    return pl.pallas_call(
        kernel,
        out_shape=jax.ShapeDtypeStruct((micros, tokens, SLICE), BF16),
        in_specs=[anywhere, vmem, vmem, vmem] + [anywhere] * 3,
        out_specs=vmem,
        scratch_shapes=[
            bf16(2, hidden_units, HALF),
            bf16(2, hidden_units, HALF),
            bf16(2, HALF, hidden_units),
            bf16(2, HALF, hidden_units),
            bf16(2, hidden_units, HALF),
            bf16(PIECES * PACKED, SOURCES * BLOCK),
            bf16(SOURCES * BLOCK, PIECES * PACKED),
            pltpu.VMEM((micros, 2, tokens), jnp.int32),
            bf16(units, tokens, HALF),
            f32(units, tokens, LANES),
            f32(units, tokens, LANES),
            f32(units, 2, tokens, LANES),
            bf16(8 * BLOCK, PIECES * tokens),
            bf16(units, 8 * BLOCK, NARROW),
            bf16(units, 2, CHIPS, BLOCK, NARROW),
            bf16(2, 2 * PACKED, HALF),
            bf16(units, 2 * PACKED, hidden_units),
            bf16(units, 2 * PACKED, hidden_units),
            f32(2 * PACKED, HALF),
            bf16(2, PIECES * PACKED, NARROW),
            bf16(units, CHIPS, BLOCK, NARROW),
            bf16(units, CHIPS, BLOCK, NARROW),
            f32(units, tokens, LANES),
            f32(units, tokens, LANES),
            bf16(PIECES * tokens, CHIPS * BLOCK),
            bf16(units, tokens, HALF),
            dma((6,)),
            dma,
            dma((units,)),
            dma((units, 2)),
            dma((units, CHIPS)),
            dma((units, CHIPS // GROUP)),
            dma((units,)),
            dma((units, CHIPS)),
            dma((units,)),
            dma((micros,)),
        ] + [dma] * 11,
        compiler_params=pltpu.CompilerParams(
            collective_id=0, has_side_effects=True, vmem_limit_bytes=60 * 2**20
        ),
        name="moe_relay",
    )(
        inputs, jnp.swapaxes(routes[0], 1, 2), norm_gain, router[0].T, w_gate[0].T, w_up[0].T,
        w_down[0],
    )


def solution(mesh):
    return jax.shard_map(
        on_device,
        mesh=mesh,
        in_specs=(
            P(None, "expert", None),
            P("section", None, "expert", None),
            P("section", None),
            P("section", None, None),
            P("section", None, "expert"),
            P("section", None, "expert"),
            P("section", "expert", None),
        ),
        out_specs=P(None, "expert", "section"),
        check_vma=False,
    )
```
